256 devices in a mesh: blk: 16 (over x, y_hi, core), narrow: 16 (over y_lo, z).
Axes of the slice: x: 4, y: 4 (y_hi: 2, y_lo: 2; y = y_hi * 2 + y_lo), z: 8, core: 2. Of those that a mesh axis runs over, the one named last changes fastest.
Arguments:
- image_emb: bfloat16 [16384, 768], P(('blk', 'narrow')), as said below
- text_emb: bfloat16 [16384, 768], P(('blk', 'narrow')), as said below
- log_temp: float32 [1], replicated, may hold values from 1 to 2
- bias: float32 [1], replicated, may hold values from -4 to -2
Outputs:
- mean_loss: float32 [1], replicated
- grad_image: float32 [16384, 768], P(('blk', 'narrow'))
- grad_text: float32 [16384, 768], P(('blk', 'narrow'))
- scalar_grads: float32 [2], replicated
The draws below stay inside these ranges and needn't reach their ends.
Inputs may be any that keep to these rules, and one draw needn't show every extreme that they name: `image_emb`: finite values. `text_emb`: finite values.
All inputs are finite; a program needn't handle non-finite values.
Results may differ from the reference program's by a relative error of at most 0.0053.
Values may be sent and summed in bfloat16 or wider, within the bound.
A program may use at most 64 MiB of HBM per device.

```python
import jax
import jax.numpy as jnp
from jax import lax

D = 768
ROWS = 64
TOTAL = 16384
N_NARROW = 16


def shared_part(key, strength):
    lead = jnp.clip(jax.random.normal(key, (TOTAL, 4), jnp.float32), -4.0, 4.0)
    lead = lead * jnp.sqrt(jnp.float32(D) / 4.0) * strength[:, None]
    return jnp.concatenate([lead, jnp.zeros((TOTAL, D - 4), jnp.float32)], 1)


def draw_image_emb(key, part):
    key = jax.random.fold_in(key, 11)
    first, second = jax.random.split(key)
    place = jnp.arange(TOTAL, dtype=jnp.float32) / jnp.float32(TOTAL - 1)
    base = jnp.clip(jax.random.normal(first, (TOTAL, D), jnp.float32), -6.0, 6.0)
    strength = 2.5 * place
    return (base + shared_part(second, strength)).astype(jnp.bfloat16)


def draw_text_emb(key, part):
    key = jax.random.fold_in(key, 12)
    first, second = jax.random.split(key)
    base = jnp.clip(jax.random.normal(first, (TOTAL, D), jnp.float32), -6.0, 6.0)
    strength = jnp.full((TOTAL,), 2.0, jnp.float32)
    return (base + shared_part(second, strength)).astype(jnp.bfloat16)


def setup_inputs(seed: int = 0) -> dict:
    streams_of = jax.random.split(jax.random.key(seed), 5)
    return {
        "image_emb": draw_image_emb(jax.random.fold_in(streams_of[4], 71), 0),
        "text_emb": draw_text_emb(jax.random.fold_in(streams_of[4], 71), 0),
        "log_temp": jnp.clip(jax.random.uniform(streams_of[2], (1,), jnp.float32, 1.0, 2.0), 1.0, 2.0),
        "bias": jnp.clip(jax.random.uniform(streams_of[3], (1,), jnp.float32, -4.0, -2.0), -4.0, -2.0),
    }


def unit_rows(values):
    widened = values.astype(jnp.float32)
    return widened * lax.rsqrt(lax.optimization_barrier(jnp.sum(widened * widened, axis=-1, keepdims=True)) + 1e-06)

def back_rows(values, upstream):
    widened = values.astype(jnp.float32)
    inverse = lax.rsqrt(lax.optimization_barrier(jnp.sum(widened * widened, axis=-1, keepdims=True)) + 1e-06)
    unit = widened * inverse
    return inverse * (upstream - unit * lax.optimization_barrier(jnp.sum(unit * upstream, axis=-1, keepdims=True)))

def reference(image_emb, text_emb, log_temp, bias):
    image_unit = unit_rows(image_emb).astype(jnp.bfloat16)
    text_unit = unit_rows(text_emb).astype(jnp.bfloat16)
    temper = jnp.exp(log_temp[0])
    offset = bias[0]
    block_rows = ROWS * N_NARROW
    block_count = TOTAL // block_rows
    image_blocks = image_unit.reshape(block_count, block_rows, D)
    text_index = jnp.arange(TOTAL, dtype=jnp.int32)

    def visit(carry, inputs):
        text_sum, running = carry
        holder, images = inputs
        image_index = holder * block_rows + jnp.arange(block_rows, dtype=jnp.int32)
        products = jnp.dot(images, text_unit.T, preferred_element_type=jnp.float32)
        logits = temper * products + offset
        matched = (image_index[:, None] == text_index[None, :]).astype(jnp.float32)
        signed = 2.0 * matched - 1.0
        loss_sum = jnp.sum(jax.nn.softplus(-signed * logits))
        slopes = jax.nn.sigmoid(logits) - matched
        found = jnp.stack([loss_sum, jnp.sum(slopes), jnp.sum(slopes * (logits - offset))])
        slopes_b = slopes.astype(jnp.bfloat16)
        image_grad = temper * jnp.dot(slopes_b, text_unit, preferred_element_type=jnp.float32)
        text_sum = text_sum + temper * jnp.dot(slopes_b.T, images, preferred_element_type=jnp.float32)
        return ((text_sum, running + found), image_grad)
    start = (jnp.zeros((TOTAL, D), jnp.float32), jnp.zeros((3,), jnp.float32))
    (text_sum, running), image_grads = lax.scan(visit, start, (jnp.arange(block_count, dtype=jnp.int32), image_blocks))
    pairs = float(TOTAL) * float(TOTAL)
    mean_loss = jnp.reshape(running[0] / pairs, (1,))
    scalar_grads = jnp.stack([running[2], running[1]]) / pairs
    grad_image = back_rows(image_emb, image_grads.reshape(TOTAL, D))
    grad_text = back_rows(text_emb, text_sum)
    return (mean_loss, grad_image, grad_text, scalar_grads)
```

```python
import math

import jax
import jax.numpy as jnp
from jax import lax
from jax.experimental import pallas as pl
from jax.experimental.pallas import tpu as pltpu
from jax.sharding import PartitionSpec as P

MESH = pl.DeviceIdType.MESH
ROWS, WIDTH = 64, 768
GROUP = 4 * ROWS
TOTAL = 16384
LOG2E = math.log2(math.e)


def ring(step, size):
    return min(step % size, -step % size)


PLANE = sorted(
    ((dx, dy) for dx in range(4) for dy in range(4)),
    key=lambda p: (ring(p[0], 4) + ring(p[1], 4), p),
)
COLUMN = sorted(range(8), key=lambda d: (ring(d, 8), d))
PLANE_BACK = [PLANE.index((-dx % 4, -dy % 4)) for dx, dy in PLANE]
COLUMN_BACK = [COLUMN.index(-d % 8) for d in COLUMN]


def text_rows(other, place):
    return (place // 2 * 4 + other * 2 + place % 2) * ROWS


def row_scale(values):
    return lax.rsqrt(jnp.sum(values * values, axis=-1, keepdims=True) + 1e-06)


def back_rows(values, upstream):
    inverse = row_scale(values)
    unit = values * inverse
    return inverse * (upstream - unit * jnp.sum(unit * upstream, axis=-1, keepdims=True))


def fold(values):
    return jnp.sum(jnp.reshape(values, (values.shape[0] // 8, 8, values.shape[1])), axis=0)


def kernel(
    image_ref, text_ref, temp_ref, bias_ref,
    grad_image_ref, grad_text_ref, scalars_ref,
    images, texts, slopes, slopes_t, sums,
    image_part, text_part, pair_part, image_own, text_own,
    image_in, text_in, pair_in, found_in, found_out,
    image_ss, image_rs, text_ss, text_rs, pair_ss, pair_rs,
    gi_ss, gi_rs, gt_ss, gt_rs, gp_ss, gp_rs, f_ss, f_rs,
):
    blk, narrow = lax.axis_index("blk"), lax.axis_index("narrow")
    x, core = lax.div(blk, 4), lax.rem(blk, 2)
    y = lax.rem(lax.div(blk, 2), 2) * 2 + lax.div(narrow, 8)
    z = lax.rem(narrow, 8)

    def device(dx, dy, dz, other):
        px, py, pz = lax.rem(x + dx, 4), lax.rem(y + dy, 4), lax.rem(z + dz, 8)
        pc = lax.rem(core + other, 2)
        return (px * 4 + lax.div(py, 2) * 2 + pc, lax.rem(py, 2) * 8 + pz)

    plane = [device(dx, dy, 0, 0) for dx, dy in PLANE]
    column = [device(0, 0, dz, 0) for dz in COLUMN]
    twin = device(0, 0, 0, 1)

    barrier = pltpu.get_barrier_semaphore()
    for peer in plane[1:] + column[1:] + [twin]:
        pl.semaphore_signal(barrier, inc=1, device_id=peer, device_id_type=MESH)

    image = image_ref[...].astype(jnp.float32)
    images[0:ROWS, :] = (image * row_scale(image)).astype(jnp.bfloat16)
    text = text_ref[...].astype(jnp.float32)
    texts[0:ROWS, :] = (text * row_scale(text)).astype(jnp.bfloat16)
    sums[...] = jnp.zeros_like(sums)
    temper = jnp.exp(jnp.full((1, 256), temp_ref[0], jnp.float32))
    offset = jnp.full((1, 256), bias_ref[0], jnp.float32)
    temper2, offset2 = temper * LOG2E, offset * LOG2E

    pl.semaphore_wait(barrier, len(plane) + len(column) - 1)

    started = []

    def send(src, dst, send_sem, recv_sem, peer):
        copy = pltpu.make_async_remote_copy(
            src_ref=src, dst_ref=dst, send_sem=send_sem, recv_sem=recv_sem,
            device_id=peer, device_id_type=MESH,
        )
        copy.start()
        started.append(copy)
        return copy

    def image_rows(place):
        return pl.ds(place * ROWS, ROWS)

    image_copies, text_copies, pair_copies = {}, {}, {}

    def send_text(place):
        back = COLUMN_BACK[place]
        text_copies[back] = send(
            texts.at[0:ROWS], texts.at[pl.ds(text_rows(0, back), ROWS)],
            text_ss.at[place], text_rs.at[back], column[place],
        )

    def send_image(place):
        back = PLANE_BACK[place]
        image_copies[back] = send(
            images.at[0:ROWS], images.at[image_rows(back)],
            image_ss.at[place], image_rs.at[back], plane[place],
        )

    def hand_text(place):
        pair_copies[place] = send(
            texts.at[pl.ds(text_rows(0, place), ROWS)], texts.at[pl.ds(text_rows(1, place), ROWS)],
            pair_ss.at[place], pair_rs.at[place], twin,
        )

    for place in range(1, 8):
        send_text(place)
        send_image(2 * place - 1)
        send_image(2 * place)
    send_image(15)
    hand_text(0)

    def tile(first, second, diagonal):
        rows = pl.ds(pl.multiple_of(first * GROUP, GROUP), GROUP)
        cols = pl.ds(pl.multiple_of(second * GROUP, GROUP), GROUP)
        products = lax.dot_general(
            images[rows, :], texts[cols, :], (((1,), (1,)), ((), ())),
            preferred_element_type=jnp.float32,
        )
        grown = jnp.exp2(products * temper2 + offset2)
        above = 1.0 + grown
        slope = grown / above
        packed = above[0:128] * above[128:256]
        packed = packed[0:64] * packed[64:128]
        packed = packed[0:32] * packed[32:64]
        loss = fold(jnp.log(packed))
        if diagonal:
            row = lax.broadcasted_iota(jnp.int32, (GROUP, GROUP), 0)
            col = lax.broadcasted_iota(jnp.int32, (GROUP, GROUP), 1)
            matched = jnp.where((row == col) & (row < ROWS), 1.0, 0.0)
            slope = slope - matched
            loss = loss - fold(matched * (products * temper + offset))
        sums[0] += loss
        sums[1] += fold(slope)
        sums[2] += fold(slope * products)
        slope = slope.astype(jnp.bfloat16)
        slopes[rows, cols] = slope
        slopes_t[cols, rows] = slope.T

    for step in range(4):
        for place in (2 * step, 2 * step + 1):
            if place:
                text_copies[place].wait_recv()
                hand_text(place)
        for place in range(4 * step, 4 * step + 4):
            if place:
                image_copies[place].wait_recv()
        for place in (2 * step, 2 * step + 1):
            pair_copies[place].wait_recv()
        if step == 0:
            tile(0, 0, True)
        else:

            def body(count, carry, step=step):
                tile(jnp.minimum(step, count), jnp.minimum(step, 2 * step - count), False)
                return carry

            lax.fori_loop(0, 2 * step + 1, body, 0)

    def spread(stage, values, peers):
        found_out[stage] = values
        return [
            send(found_out.at[stage], found_in.at[stage, n], f_ss.at[stage, n], f_rs.at[stage, n], peer)
            for n, peer in enumerate(peers)
        ]

    def collect(stage, values, copies):
        for n, copy in enumerate(copies):
            copy.wait_recv()
            values = values + found_in[stage, n]
        return values

    lane_sums = [jnp.sum(sums[n], keepdims=True) for n in range(3)]
    row = lax.broadcasted_iota(jnp.int32, (8, 128), 0)
    found = jnp.where(row == 0, lane_sums[0], jnp.where(row == 1, lane_sums[1], lane_sums[2]))
    found_copies = spread(0, found, plane[1:])

    gi_copies, gt_copies, gp_copies = {}, {}, {}
    temper3 = jnp.concatenate([temper] * 3, axis=1)

    def image_grads(group):
        rows = slice(group * GROUP, group * GROUP + GROUP)
        part = temper3 * jnp.dot(slopes[rows, :], texts[...], preferred_element_type=jnp.float32)
        image_part[rows, :] = part.astype(jnp.bfloat16)
        if group == 0:
            image_own[...] = part[0:ROWS]
        for place in range(4 * group, 4 * group + 4):
            if place:
                back = PLANE_BACK[place]
                gi_copies[back] = send(
                    image_part.at[image_rows(place)], image_in.at[back],
                    gi_ss.at[place], gi_rs.at[back], plane[place],
                )

    def text_grads(group):
        rows = slice(group * GROUP, group * GROUP + GROUP)
        part = temper3 * jnp.dot(slopes_t[rows, :], images[...], preferred_element_type=jnp.float32)
        own = slice(2 * group * ROWS, 2 * group * ROWS + 2 * ROWS)
        text_own[own, :] = part[0 : 2 * ROWS]
        pair_part[own, :] = part[2 * ROWS : 4 * ROWS].astype(jnp.bfloat16)
        gp_copies[group] = send(
            pair_part.at[own], pair_in.at[own], gp_ss.at[group], gp_rs.at[group], twin
        )

    def text_sums(group):
        gp_copies[group].wait_recv()
        for place in (2 * group + 1, 2 * group):
            own = slice(place * ROWS, place * ROWS + ROWS)
            part = text_own[own, :] + pair_in[own, :].astype(jnp.float32)
            if place == 0:
                text_own[own, :] = part
            else:
                back = COLUMN_BACK[place]
                text_part[own, :] = part.astype(jnp.bfloat16)
                gt_copies[back] = send(
                    text_part.at[own], text_in.at[back], gt_ss.at[place], gt_rs.at[back], column[place]
                )

    text_grads(3)
    image_grads(3)
    text_sums(3)
    text_grads(2)
    found = collect(0, found, found_copies)
    found_copies = spread(1, found, column[1:])
    image_grads(2)
    text_sums(2)
    text_grads(1)
    found = collect(1, found, found_copies)
    found_copies = spread(2, found, [twin])
    image_grads(1)
    text_sums(1)
    text_grads(0)
    image_grads(0)
    text_sums(0)

    found = collect(2, found, found_copies) * (1.0 / float(TOTAL) ** 2)
    scalars_ref[...] = jnp.where(row == 2, found * temper[:, 0:128], found)

    total = text_own[0:ROWS, :]
    for place in range(7, 0, -1):
        gt_copies[place].wait_recv()
        total = total + text_in[place].astype(jnp.float32)
    grad_text_ref[...] = back_rows(text_ref[...].astype(jnp.float32), total)

    total = image_own[...]
    for place in range(15, 0, -1):
        gi_copies[place].wait_recv()
        total = total + image_in[place].astype(jnp.float32)
    grad_image_ref[...] = back_rows(image_ref[...].astype(jnp.float32), total)

    for copy in started:
        copy.wait_send()


def local(image_emb, text_emb, log_temp, bias):
    bf16, f32 = jnp.bfloat16, jnp.float32
    vmem, smem = pl.BlockSpec(memory_space=pltpu.VMEM), pl.BlockSpec(memory_space=pltpu.SMEM)
    dma = pltpu.SemaphoreType.DMA
    grad_image, grad_text, scalars = pl.pallas_call(
        kernel,
        out_shape=(
            jax.ShapeDtypeStruct((ROWS, WIDTH), f32),
            jax.ShapeDtypeStruct((ROWS, WIDTH), f32),
            jax.ShapeDtypeStruct((8, 128), f32),
        ),
        in_specs=[vmem, vmem, smem, smem],
        out_specs=(vmem, vmem, vmem),
        scratch_shapes=[
            pltpu.VMEM((16 * ROWS, WIDTH), bf16),
            pltpu.VMEM((16 * ROWS, WIDTH), bf16),
            pltpu.VMEM((16 * ROWS, 16 * ROWS), bf16),
            pltpu.VMEM((16 * ROWS, 16 * ROWS), bf16),
            pltpu.VMEM((3, 8, 256), f32),
            pltpu.VMEM((16 * ROWS, WIDTH), bf16),
            pltpu.VMEM((8 * ROWS, WIDTH), bf16),
            pltpu.VMEM((8 * ROWS, WIDTH), bf16),
            pltpu.VMEM((ROWS, WIDTH), f32),
            pltpu.VMEM((8 * ROWS, WIDTH), f32),
            pltpu.VMEM((16, ROWS, WIDTH), bf16),
            pltpu.VMEM((8, ROWS, WIDTH), bf16),
            pltpu.VMEM((8 * ROWS, WIDTH), bf16),
            pltpu.VMEM((3, 15, 8, 128), f32),
            pltpu.VMEM((3, 8, 128), f32),
            dma((16,)), dma((16,)), dma((8,)), dma((8,)), dma((8,)), dma((8,)),
            dma((16,)), dma((16,)), dma((8,)), dma((8,)), dma((4,)), dma((4,)),
            dma((3, 15)), dma((3, 15)),
        ],
        compiler_params=pltpu.CompilerParams(
            collective_id=0, has_side_effects=True, vmem_limit_bytes=40 * 1024 * 1024
        ),
    )(image_emb, text_emb, log_temp, bias)
    return (scalars[0, 0:1], grad_image, grad_text, jnp.stack([scalars[2, 0], scalars[1, 0]]))


def solution(mesh):
    placed = (P(("blk", "narrow"), None), P(("blk", "narrow"), None), P(), P())
    return jax.shard_map(
        local,
        mesh=mesh,
        in_specs=placed,
        out_specs=(P(), P(("blk", "narrow"), None), P(("blk", "narrow"), None), P()),
        check_vma=False,
    )
```

```python
import math

import jax
import jax.numpy as jnp
from jax import lax
from jax.experimental import pallas as pl
from jax.experimental.pallas import tpu as pltpu
from jax.sharding import PartitionSpec as P

MESH = pl.DeviceIdType.MESH
ROWS, WIDTH = 64, 768
HALF, LINE, GROUP = ROWS // 2, 2 * ROWS, 4 * ROWS
TOTAL = 16384
LOG2E = math.log2(math.e)

AROUND = (0, 1, 3, 2)
AROUND_BACK = tuple(AROUND.index(-d % 4) for d in AROUND)
COLUMN = (0, 1, 7, 6, 2, 4, 3, 5)
COLUMN_BACK = tuple(COLUMN.index(-d % 8) for d in COLUMN)


def image_row(half, line, place):
    return line * GROUP + half * LINE + place * HALF


def text_row(other, place):
    return (place // 2 * 4 + other * 2 + place % 2) * ROWS


def row_scale(values):
    return lax.rsqrt(jnp.sum(values * values, axis=-1, keepdims=True) + 1e-06)


def back_rows(values, upstream):
    inverse = row_scale(values)
    unit = values * inverse
    return inverse * (upstream - unit * jnp.sum(unit * upstream, axis=-1, keepdims=True))


def fold(values):
    return jnp.sum(jnp.reshape(values, (values.shape[0] // 8, 8, values.shape[1])), axis=0)


def wide(ref):
    return ref.astype(jnp.float32)


def kernel(
    image_hbm, text_hbm, temp_ref, bias_ref,
    grad_image_ref, grad_text_ref, scalars_ref,
    image_ref, text_ref, images, texts, slopes, slopes_t, sums,
    image_part, image_own, image_in, image_mid, image_last,
    text_part, text_own, text_in, pair_part, pair_in, text_mid, found_in, found_out,
    load, image_ss, image_rs, text_ss, text_rs, pair_ss, pair_rs,
    line_ss, line_rs, last_ss, last_rs, gt_ss, gt_rs, mid_ss, mid_rs, gp_ss, gp_rs, f_ss, f_rs,
):
    blk, narrow = lax.axis_index("blk"), lax.axis_index("narrow")
    x, core = lax.div(blk, 4), lax.rem(blk, 2)
    y = lax.rem(lax.div(blk, 2), 2) * 2 + lax.div(narrow, 8)
    z = lax.rem(narrow, 8)

    def device(dx, dy, dz, other):
        px, py, pz = lax.rem(x + dx, 4), lax.rem(y + dy, 4), lax.rem(z + dz, 8)
        pc = lax.rem(core + other, 2)
        return (px * 4 + lax.div(py, 2) * 2 + pc, lax.rem(py, 2) * 8 + pz)

    axes = ([device(d, 0, 0, 0) for d in AROUND], [device(0, d, 0, 0) for d in AROUND])
    column = {d: device(0, 0, d, 0) for d in range(1, 8)}
    twin = device(0, 0, 0, 1)

    barrier = pltpu.get_barrier_semaphore()
    peers = [axes[0][3], axes[1][3], *axes[0][1:3], *axes[1][1:3], *column.values(), twin]
    for peer in peers:
        pl.semaphore_signal(barrier, inc=1, device_id=peer, device_id_type=MESH)
    loads = [
        pltpu.make_async_copy(image_hbm, image_ref, load.at[0]),
        pltpu.make_async_copy(text_hbm, text_ref, load.at[1]),
    ]
    for copy in loads:
        copy.start()
    sums[...] = jnp.zeros_like(sums)
    temper = jnp.exp(jnp.full((1, 256), temp_ref[0], jnp.float32))
    offset = jnp.full((1, 256), bias_ref[0], jnp.float32)
    temper2, offset2 = temper * LOG2E, offset * LOG2E
    temper3 = jnp.concatenate([temper] * 3, axis=1)
    for copy in loads:
        copy.wait()
    image = wide(image_ref[...])
    image = (image * row_scale(image)).astype(jnp.bfloat16)
    for half in (0, 1):
        row = image_row(half, 0, 0)
        images[row : row + HALF, :] = image[half * HALF : half * HALF + HALF]
    text = wide(text_ref[...])
    texts[0:ROWS, :] = (text * row_scale(text)).astype(jnp.bfloat16)

    pl.semaphore_wait(barrier, len(peers))

    started = []

    def send(src, dst, send_sem, recv_sem, peer):
        copy = pltpu.make_async_remote_copy(
            src_ref=src, dst_ref=dst, send_sem=send_sem, recv_sem=recv_sem,
            device_id=peer, device_id_type=MESH,
        )
        copy.start()
        started.append(copy)
        return copy

    image_copies, text_copies, pair_copies = {}, {}, {}

    def first_image(half, place):
        back = AROUND_BACK[place]
        image_copies[half, 0, back] = send(
            images.at[pl.ds(image_row(half, 0, 0), HALF)],
            images.at[pl.ds(image_row(half, 0, back), HALF)],
            image_ss.at[half, 0, place], image_rs.at[half, 0, back], axes[half][place],
        )

    def pass_image(half, place):
        for line in (3, 1, 2):
            back = AROUND_BACK[line]
            image_copies[half, back, place] = send(
                images.at[pl.ds(image_row(half, 0, place), HALF)],
                images.at[pl.ds(image_row(half, back, place), HALF)],
                image_ss.at[half, line, place], image_rs.at[half, back, place], axes[1 - half][line],
            )

    def send_text(block, step, first, count, slot):
        source, target = text_row(0, COLUMN.index(block)), text_row(0, COLUMN.index((block - step) % 8))
        text_copies[(block - step) % 8, first] = send(
            texts.at[pl.ds(source + first, count)], texts.at[pl.ds(target + first, count)],
            text_ss.at[slot], text_rs.at[slot], column[step % 8],
        )

    def hand_text(block):
        place = COLUMN.index(block)
        pair_copies[block] = send(
            texts.at[pl.ds(text_row(0, place), ROWS)], texts.at[pl.ds(text_row(1, place), ROWS)],
            pair_ss.at[place], pair_rs.at[place], twin,
        )

    send_text(0, 2, 0, ROWS, 0)
    send_text(0, -2, 0, ROWS, 1)
    for place in (3, 1, 2):
        for half in (0, 1):
            first_image(half, place)
    send_text(0, 1, 0, ROWS, 2)
    send_text(0, -1, 0, ROWS, 3)
    hand_text(0)
    for half in (0, 1):
        pass_image(half, 0)
    for place in (1, 2, 3):
        for half in (0, 1):
            image_copies[half, 0, place].wait_recv()
            pass_image(half, place)
    text_copies[2, 0].wait_recv()
    send_text(2, -1, 0, ROWS, 4)
    send_text(2, -2, 0, HALF, 5)
    text_copies[6, 0].wait_recv()
    send_text(6, 1, 0, ROWS, 6)
    send_text(6, 2, HALF, HALF, 7)
    hand_text(2)
    hand_text(6)

    def tile(first, second, diagonal):
        rows = pl.ds(pl.multiple_of(first * GROUP, GROUP), GROUP)
        cols = pl.ds(pl.multiple_of(second * GROUP, GROUP), GROUP)
        products = lax.dot_general(
            images[rows, :], texts[cols, :], (((1,), (1,)), ((), ())),
            preferred_element_type=jnp.float32,
        )
        grown = jnp.exp2(products * temper2 + offset2)
        above = 1.0 + grown
        slope = grown / above
        packed = above[0:128] * above[128:256]
        packed = packed[0:64] * packed[64:128]
        packed = packed[0:32] * packed[32:64]
        loss = fold(jnp.log(packed))
        if diagonal:
            row = lax.broadcasted_iota(jnp.int32, (GROUP, GROUP), 0)
            col = lax.broadcasted_iota(jnp.int32, (GROUP, GROUP), 1)
            upper = (row == col) & (row < HALF)
            lower = (row - LINE + HALF == col) & (row >= LINE) & (row < LINE + HALF)
            matched = jnp.where(upper | lower, 1.0, 0.0)
            slope = slope - matched
            loss = loss - fold(matched * (products * temper + offset))
        sums[0] += loss
        sums[1] += fold(slope)
        sums[2] += fold(slope * products)
        slope = slope.astype(jnp.bfloat16)
        slopes[rows, cols] = slope
        slopes_t[cols, rows] = slope.T

    def tiles(firsts, seconds):
        count = seconds[1] - seconds[0]

        def body(n, carry):
            tile(firsts[0] + lax.div(n, count), seconds[0] + lax.rem(n, count), False)
            return carry

        lax.fori_loop(0, (firsts[1] - firsts[0]) * count, body, 0)

    def wait_lines(line):
        for half in (0, 1):
            for place in range(4):
                image_copies[half, line, place].wait_recv()

    for block in (1, 7):
        text_copies[block, 0].wait_recv()
        hand_text(block)
    for block in (0, 1):
        pair_copies[block].wait_recv()
    tile(0, 0, True)
    for block in (6, 7):
        pair_copies[block].wait_recv()
    tiles((0, 1), (1, 2))
    wait_lines(1)
    wait_lines(2)
    tiles((1, 3), (0, 2))
    for block in (3, 5):
        text_copies[block, 0].wait_recv()
        hand_text(block)
    wait_lines(3)
    tiles((3, 4), (0, 2))
    for first in (0, HALF):
        text_copies[4, first].wait_recv()
    hand_text(4)
    for block in (3, 5):
        pair_copies[block].wait_recv()
    tiles((0, 4), (3, 4))
    for block in (2, 4):
        pair_copies[block].wait_recv()
    tiles((0, 4), (2, 3))

    def spread(stage, values, peers):
        found_out[stage] = values
        return [
            send(found_out.at[stage], found_in.at[stage, n], f_ss.at[stage, n], f_rs.at[stage, n], peer)
            for n, peer in enumerate(peers)
        ]

    def collect(stage, values, copies):
        for n, copy in enumerate(copies):
            copy.wait_recv()
            values = values + found_in[stage, n]
        return values

    lane_sums = [jnp.sum(sums[n], keepdims=True) for n in range(3)]
    row = lax.broadcasted_iota(jnp.int32, (8, 128), 0)
    found = jnp.where(row == 0, lane_sums[0], jnp.where(row == 1, lane_sums[1], lane_sums[2]))
    found_copies = spread(0, found, axes[0][1:])

    line_copies, last_copies, gt_copies, mid_copies, gp_copies = {}, {}, {}, {}, {}

    def image_grads(line):
        rows = slice(line * GROUP, line * GROUP + GROUP)
        part = temper3 * jnp.dot(slopes[rows, :], texts[...], preferred_element_type=jnp.float32)
        if line == 0:
            image_own[...] = part
        else:
            image_part[rows, :] = part.astype(jnp.bfloat16)

    def send_lines(line, own):
        first, count = (0, HALF) if own else (HALF, LINE - HALF)
        back = AROUND_BACK[line]
        for half in (0, 1):
            line_copies[half, back, own] = send(
                image_part.at[pl.ds(image_row(half, line, 0) + first, count)],
                image_in.at[half, back, pl.ds(first, count)],
                line_ss.at[half, line, own], line_rs.at[half, back, own], axes[1 - half][line],
            )

    def line_sum(half, own):
        first, count = (0, HALF) if own else (HALF, LINE - HALF)
        row = half * LINE + first
        part = image_own[row : row + count, :]
        for line in (3, 1, 2):
            line_copies[half, line, own].wait_recv()
            part = part + wide(image_in[half, line, first : first + count, :])
        return part

    def text_grads(group):
        rows = slice(group * GROUP, group * GROUP + GROUP)
        part = temper3 * jnp.dot(slopes_t[rows, :], images[...], preferred_element_type=jnp.float32)
        own = slice(group * LINE, group * LINE + LINE)
        text_own[own, :] = part[0:LINE]
        pair_part[own, :] = part[LINE:GROUP].astype(jnp.bfloat16)
        gp_copies[group] = send(
            pair_part.at[own], pair_in.at[own], gp_ss.at[group], gp_rs.at[group], twin
        )

    def own_rows(block, first=0, count=ROWS):
        place = COLUMN.index(block)
        return slice(place * ROWS + first, place * ROWS + first + count)

    def text_sums(group):
        gp_copies[group].wait_recv()
        own = slice(group * LINE, group * LINE + LINE)
        part = text_own[own, :] + wide(pair_in[own, :])
        text_own[own, :] = part
        text_part[own, :] = part.astype(jnp.bfloat16)

    def send_mid(block, step, first, count, slot):
        mid_copies[slot] = send(
            text_part.at[own_rows(block, first, count)], text_mid.at[slot, pl.ds(first, count)],
            mid_ss.at[slot], mid_rs.at[slot], column[step % 8],
        )

    def send_share(block, slot):
        gt_copies[slot] = send(
            text_part.at[own_rows(block)], text_in.at[slot], gt_ss.at[slot], gt_rs.at[slot], column[block]
        )

    def add_mid(block, near, far, first, slot):
        mid_copies[near].wait_recv()
        part = text_own[own_rows(block), :] + wide(text_mid[near])
        mid_copies[far].wait_recv()
        more = part[first : first + HALF] + wide(text_mid[far, first : first + HALF, :])
        part = jnp.concatenate([more, part[HALF:]] if first == 0 else [part[:HALF], more], axis=0)
        text_part[own_rows(block), :] = part.astype(jnp.bfloat16)
        send_share(block, slot)

    text_grads(3)
    image_grads(3)
    send_lines(3, 0)
    send_lines(3, 1)
    text_sums(3)
    send_mid(3, 1, 0, ROWS, 0)
    send_mid(5, -1, 0, ROWS, 1)
    text_grads(2)
    image_grads(1)
    send_lines(1, 0)
    text_sums(2)
    send_mid(4, 2, 0, HALF, 2)
    send_mid(4, -2, HALF, HALF, 3)
    text_grads(1)
    image_grads(2)
    send_lines(2, 0)
    send_lines(1, 1)
    send_lines(2, 1)
    text_sums(1)
    send_share(7, 0)
    found = collect(0, found, found_copies)
    found_copies = spread(1, found, axes[1][1:])
    text_grads(0)
    image_grads(0)
    text_sums(0)
    send_share(1, 1)
    add_mid(2, 0, 2, 0, 2)
    add_mid(6, 1, 3, HALF, 3)
    found = collect(1, found, found_copies)
    found_copies = spread(2, found, list(column.values()))

    for half in (0, 1):
        part = line_sum(half, 0).astype(jnp.bfloat16)
        image_mid[half] = part
        for place in (3, 1, 2):
            back = AROUND_BACK[place]
            last_copies[half, back] = send(
                image_mid.at[half, pl.ds(place * HALF - HALF, HALF)], image_last.at[half, back],
                last_ss.at[half, place], last_rs.at[half, back], axes[half][place],
            )
    found = collect(2, found, found_copies)
    found_copies = spread(3, found, [twin])
    ends = [line_sum(half, 1) for half in (0, 1)]

    total = text_own[0:ROWS, :]
    for slot in range(4):
        gt_copies[slot].wait_recv()
        total = total + wide(text_in[slot])
    grad_text_ref[...] = back_rows(wide(text_ref[...]), total)

    found = collect(3, found, found_copies) * (1.0 / float(TOTAL) ** 2)
    scalars_ref[...] = jnp.where(row == 2, found * temper[:, 0:128], found)

    for half in (0, 1):
        total = ends[half]
        for place in (1, 2, 3):
            last_copies[half, place].wait_recv()
            total = total + wide(image_last[half, place])
        rows = slice(half * HALF, half * HALF + HALF)
        grad_image_ref[rows, :] = back_rows(wide(image_ref[rows, :]), total)

    for copy in started:
        copy.wait_send()


def local(image_emb, text_emb, log_temp, bias):
    bf16, f32 = jnp.bfloat16, jnp.float32
    vmem, smem = pl.BlockSpec(memory_space=pltpu.VMEM), pl.BlockSpec(memory_space=pltpu.SMEM)
    hbm = pl.BlockSpec(memory_space=pl.ANY)
    dma = pltpu.SemaphoreType.DMA
    grad_image, grad_text, scalars = pl.pallas_call(
        kernel,
        out_shape=(
            jax.ShapeDtypeStruct((ROWS, WIDTH), f32),
            jax.ShapeDtypeStruct((ROWS, WIDTH), f32),
            jax.ShapeDtypeStruct((8, 128), f32),
        ),
        in_specs=[hbm, hbm, smem, smem],
        out_specs=(vmem, vmem, vmem),
        scratch_shapes=[
            pltpu.VMEM((ROWS, WIDTH), bf16),
            pltpu.VMEM((ROWS, WIDTH), bf16),
            pltpu.VMEM((16 * ROWS, WIDTH), bf16),
            pltpu.VMEM((16 * ROWS, WIDTH), bf16),
            pltpu.VMEM((16 * ROWS, 16 * ROWS), bf16),
            pltpu.VMEM((16 * ROWS, 16 * ROWS), bf16),
            pltpu.VMEM((3, 8, 256), f32),
            pltpu.VMEM((16 * ROWS, WIDTH), bf16),
            pltpu.VMEM((GROUP, WIDTH), f32),
            pltpu.VMEM((2, 4, LINE, WIDTH), bf16),
            pltpu.VMEM((2, LINE - HALF, WIDTH), bf16),
            pltpu.VMEM((2, 4, HALF, WIDTH), bf16),
            pltpu.VMEM((8 * ROWS, WIDTH), bf16),
            pltpu.VMEM((8 * ROWS, WIDTH), f32),
            pltpu.VMEM((4, ROWS, WIDTH), bf16),
            pltpu.VMEM((8 * ROWS, WIDTH), bf16),
            pltpu.VMEM((8 * ROWS, WIDTH), bf16),
            pltpu.VMEM((4, ROWS, WIDTH), bf16),
            pltpu.VMEM((4, 7, 8, 128), f32),
            pltpu.VMEM((4, 8, 128), f32),
            dma((2,)),
            dma((2, 4, 4)), dma((2, 4, 4)), dma((8,)), dma((8,)), dma((8,)), dma((8,)),
            dma((2, 4, 2)), dma((2, 4, 2)), dma((2, 4)), dma((2, 4)),
            dma((4,)), dma((4,)), dma((4,)), dma((4,)), dma((4,)), dma((4,)),
            dma((4, 7)), dma((4, 7)),
        ],
        compiler_params=pltpu.CompilerParams(
            collective_id=0, has_side_effects=True, vmem_limit_bytes=56 * 1024 * 1024
        ),
    )(image_emb, text_emb, log_temp, bias)
    return (scalars[0, 0:1], grad_image, grad_text, jnp.stack([scalars[2, 0], scalars[1, 0]]))


def solution(mesh):
    placed = (P(("blk", "narrow"), None), P(("blk", "narrow"), None), P(), P())
    return jax.shard_map(
        local,
        mesh=mesh,
        in_specs=placed,
        out_specs=(P(), P(("blk", "narrow"), None), P(("blk", "narrow"), None), P()),
        check_vma=False,
    )
```

```python
import math

import jax
import jax.numpy as jnp
from jax import lax
from jax.experimental import pallas as pl
from jax.experimental.pallas import tpu as pltpu
from jax.sharding import PartitionSpec as P

MESH = pl.DeviceIdType.MESH
ROWS, WIDTH = 64, 768
HALF, LINE, GROUP = ROWS // 2, 2 * ROWS, 4 * ROWS
TOTAL = 16384
LOG2E = math.log2(math.e)

AROUND = (0, 1, 3, 2)
AROUND_BACK = tuple(AROUND.index(-d % 4) for d in AROUND)
COLUMN = (0, 1, 7, 6, 2, 4, 3, 5)
COLUMN_BACK = tuple(COLUMN.index(-d % 8) for d in COLUMN)


def image_row(half, line, place):
    return line * GROUP + half * LINE + place * HALF


def text_row(other, place):
    return (place // 2 * 4 + other * 2 + place % 2) * ROWS


def row_scale(values):
    return lax.rsqrt(jnp.sum(values * values, axis=-1, keepdims=True) + 1e-06)


def back_rows(values, upstream):
    inverse = row_scale(values)
    unit = values * inverse
    return inverse * (upstream - unit * jnp.sum(unit * upstream, axis=-1, keepdims=True))


def fold(values):
    return jnp.sum(jnp.reshape(values, (values.shape[0] // 8, 8, values.shape[1])), axis=0)


def wide(ref):
    return ref.astype(jnp.float32)


def kernel(
    image_hbm, text_hbm, temp_hbm, bias_hbm,
    total_image_ref, total_text_ref, scalars_ref,
    temp_ref, bias_ref, image_ref, text_ref, images, texts, texts_t, slopes, slopes_t, sums,
    image_part, image_own, image_in, image_mid, image_last,
    text_part, text_own, text_in, pair_part, pair_in, text_mid, found_in, found_out,
    load, image_ss, image_rs, text_ss, text_rs, pair_ss, pair_rs,
    line_ss, line_rs, last_ss, last_rs, gt_ss, gt_rs, mid_ss, mid_rs, gp_ss, gp_rs, f_ss, f_rs,
):
    blk, narrow = lax.axis_index("blk"), lax.axis_index("narrow")
    x, core = lax.div(blk, 4), lax.rem(blk, 2)
    y = lax.rem(lax.div(blk, 2), 2) * 2 + lax.div(narrow, 8)
    z = lax.rem(narrow, 8)

    def device(dx, dy, dz, other):
        px, py, pz = lax.rem(x + dx, 4), lax.rem(y + dy, 4), lax.rem(z + dz, 8)
        pc = lax.rem(core + other, 2)
        return (px * 4 + lax.div(py, 2) * 2 + pc, lax.rem(py, 2) * 8 + pz)

    axes = ([device(d, 0, 0, 0) for d in AROUND], [device(0, d, 0, 0) for d in AROUND])
    column = {d: device(0, 0, d, 0) for d in range(1, 8)}
    twin = device(0, 0, 0, 1)

    barrier = pltpu.get_barrier_semaphore()
    peers = [axes[0][3], axes[1][3], *axes[0][1:3], *axes[1][1:3], *column.values(), twin]
    for peer in peers:
        pl.semaphore_signal(barrier, inc=1, device_id=peer, device_id_type=MESH)
    loads = [
        pltpu.make_async_copy(image_hbm, image_ref, load.at[0]),
        pltpu.make_async_copy(text_hbm, text_ref, load.at[1]),
        pltpu.make_async_copy(temp_hbm, temp_ref, load.at[2]),
        pltpu.make_async_copy(bias_hbm, bias_ref, load.at[3]),
    ]
    for copy in loads:
        copy.start()
    sums[...] = jnp.zeros_like(sums)
    for copy in loads:
        copy.wait()
    temper = jnp.exp(jnp.full((1, 256), temp_ref[0], jnp.float32))
    offset = jnp.full((1, 256), bias_ref[0], jnp.float32)
    temper2, offset2 = temper * LOG2E, offset * LOG2E
    temper3 = jnp.concatenate([temper] * 3, axis=1)
    image = wide(image_ref[...])
    image = (image * row_scale(image)).astype(jnp.bfloat16)
    for half in (0, 1):
        row = image_row(half, 0, 0)
        images[row : row + HALF, :] = image[half * HALF : half * HALF + HALF]
    text = wide(text_ref[...])
    texts[0:ROWS, :] = (text * row_scale(text)).astype(jnp.bfloat16)

    pl.semaphore_wait(barrier, len(peers))

    started = []

    def send(src, dst, send_sem, recv_sem, peer):
        copy = pltpu.make_async_remote_copy(
            src_ref=src, dst_ref=dst, send_sem=send_sem, recv_sem=recv_sem,
            device_id=peer, device_id_type=MESH,
        )
        copy.start()
        started.append(copy)
        return copy

    image_copies, text_copies, pair_copies = {}, {}, {}

    def first_image(half, place):
        back = AROUND_BACK[place]
        image_copies[half, 0, back] = send(
            images.at[pl.ds(image_row(half, 0, 0), HALF)],
            images.at[pl.ds(image_row(half, 0, back), HALF)],
            image_ss.at[half, 0, place], image_rs.at[half, 0, back], axes[half][place],
        )

    def pass_image(half, place):
        for line in (3, 1, 2):
            back = AROUND_BACK[line]
            image_copies[half, back, place] = send(
                images.at[pl.ds(image_row(half, 0, place), HALF)],
                images.at[pl.ds(image_row(half, back, place), HALF)],
                image_ss.at[half, line, place], image_rs.at[half, back, place], axes[1 - half][line],
            )

    def send_text(block, step, first, count, slot):
        source, target = text_row(0, COLUMN.index(block)), text_row(0, COLUMN.index((block - step) % 8))
        text_copies[(block - step) % 8, first] = send(
            texts.at[pl.ds(source + first, count)], texts.at[pl.ds(target + first, count)],
            text_ss.at[slot], text_rs.at[slot], column[step % 8],
        )

    def hand_text(block):
        place = COLUMN.index(block)
        pair_copies[block] = send(
            texts.at[pl.ds(text_row(0, place), ROWS)], texts.at[pl.ds(text_row(1, place), ROWS)],
            pair_ss.at[place], pair_rs.at[place], twin,
        )

    send_text(0, 2, 0, ROWS, 0)
    send_text(0, -2, 0, ROWS, 1)
    for place in (3, 1, 2):
        for half in (0, 1):
            first_image(half, place)
    send_text(0, 1, 0, ROWS, 2)
    send_text(0, -1, 0, ROWS, 3)
    hand_text(0)
    for half in (0, 1):
        pass_image(half, 0)
    for place in (1, 2, 3):
        for half in (0, 1):
            image_copies[half, 0, place].wait_recv()
            pass_image(half, place)
    text_copies[2, 0].wait_recv()
    send_text(2, -1, 0, ROWS, 4)
    send_text(2, -2, 0, HALF, 5)
    text_copies[6, 0].wait_recv()
    send_text(6, 1, 0, ROWS, 6)
    send_text(6, 2, HALF, HALF, 7)
    hand_text(2)
    hand_text(6)

    def pairs(products, first, second):
        rows = slice(first * GROUP, first * GROUP + GROUP)
        cols = slice(second * GROUP, second * GROUP + GROUP)
        grown = jnp.exp2(products * temper2 + offset2)
        above = 1.0 + grown
        slope = grown / above
        packed = above[0:128] * above[128:256]
        packed = packed[0:64] * packed[64:128]
        packed = packed[0:32] * packed[32:64]
        loss = fold(jnp.log(packed))
        if first == 0 and second == 0:
            row = lax.broadcasted_iota(jnp.int32, (GROUP, GROUP), 0)
            col = lax.broadcasted_iota(jnp.int32, (GROUP, GROUP), 1)
            upper = (row == col) & (row < HALF)
            lower = (row - LINE + HALF == col) & (row >= LINE) & (row < LINE + HALF)
            matched = jnp.where(upper | lower, 1.0, 0.0)
            slope = slope - matched
            loss = loss - fold(matched * (products * temper + offset))
        slope_b = slope.astype(jnp.bfloat16)
        slopes[rows, cols] = slope_b
        slopes_t[cols, rows] = slope_b.T
        return loss, fold(slope), fold(slope * products)

    def tiles(*places):
        products = [
            jnp.dot(
                images[first * GROUP : first * GROUP + GROUP, :],
                texts_t[:, second * GROUP : second * GROUP + GROUP],
                preferred_element_type=jnp.float32,
            )
            for first, second in places
        ]
        shares = [pairs(product, *place) for product, place in zip(products, places)]
        for n in range(3):
            sums[n] += sum(share[n] for share in shares)

    def wait_lines(line):
        for half in (0, 1):
            for place in range(4):
                image_copies[half, line, place].wait_recv()

    def turn_texts(group):
        for block in COLUMN[2 * group : 2 * group + 2]:
            pair_copies[block].wait_recv()
        rows = slice(group * GROUP, group * GROUP + GROUP)
        texts_t[:, rows] = texts[rows, :].T

    def spread(stage, values, peers):
        found_out[stage] = values
        return [
            send(found_out.at[stage], found_in.at[stage, n], f_ss.at[stage, n], f_rs.at[stage, n], peer)
            for n, peer in enumerate(peers)
        ]

    def collect(stage, values, copies):
        for n, copy in enumerate(copies):
            copy.wait_recv()
            values = values + found_in[stage, n]
        return values

    row = lax.broadcasted_iota(jnp.int32, (8, 128), 0)
    line_copies, last_copies, gt_copies, mid_copies, gp_copies = {}, {}, {}, {}, {}

    def image_grads(line):
        rows = slice(line * GROUP, line * GROUP + GROUP)
        part = temper3 * jnp.dot(slopes[rows, :], texts[...], preferred_element_type=jnp.float32)
        if line == 0:
            image_own[...] = part
        else:
            image_part[rows, :] = part.astype(jnp.bfloat16)

    def send_lines(line, own):
        first, count = (0, HALF) if own else (HALF, LINE - HALF)
        back = AROUND_BACK[line]
        for half in (0, 1):
            line_copies[half, back, own] = send(
                image_part.at[pl.ds(image_row(half, line, 0) + first, count)],
                image_in.at[half, back, pl.ds(first, count)],
                line_ss.at[half, line, own], line_rs.at[half, back, own], axes[1 - half][line],
            )

    def line_sum(half, own):
        first, count = (0, HALF) if own else (HALF, LINE - HALF)
        row = half * LINE + first
        part = image_own[row : row + count, :]
        for line in (3, 1, 2):
            line_copies[half, line, own].wait_recv()
            part = part + wide(image_in[half, line, first : first + count, :])
        return part

    def text_grads(group):
        rows = slice(group * GROUP, group * GROUP + GROUP)
        part = temper3 * jnp.dot(slopes_t[rows, :], images[...], preferred_element_type=jnp.float32)
        own = slice(group * LINE, group * LINE + LINE)
        text_own[own, :] = part[0:LINE]
        pair_part[own, :] = part[LINE:GROUP].astype(jnp.bfloat16)
        gp_copies[group] = send(
            pair_part.at[own], pair_in.at[own], gp_ss.at[group], gp_rs.at[group], twin
        )

    def own_rows(block, first=0, count=ROWS):
        place = COLUMN.index(block)
        return slice(place * ROWS + first, place * ROWS + first + count)

    def text_sums(group):
        gp_copies[group].wait_recv()
        own = slice(group * LINE, group * LINE + LINE)
        part = text_own[own, :] + wide(pair_in[own, :])
        text_own[own, :] = part
        text_part[own, :] = part.astype(jnp.bfloat16)

    def send_mid(block, step, first, count, slot):
        mid_copies[slot] = send(
            text_part.at[own_rows(block, first, count)], text_mid.at[slot, pl.ds(first, count)],
            mid_ss.at[slot], mid_rs.at[slot], column[step % 8],
        )

    def send_share(block, slot):
        gt_copies[slot] = send(
            text_part.at[own_rows(block)], text_in.at[slot], gt_ss.at[slot], gt_rs.at[slot], column[block]
        )

    def add_mid(block, near, far, first, slot):
        mid_copies[near].wait_recv()
        part = text_own[own_rows(block), :] + wide(text_mid[near])
        mid_copies[far].wait_recv()
        more = part[first : first + HALF] + wide(text_mid[far, first : first + HALF, :])
        part = jnp.concatenate([more, part[HALF:]] if first == 0 else [part[:HALF], more], axis=0)
        text_part[own_rows(block), :] = part.astype(jnp.bfloat16)
        send_share(block, slot)

    for block in (1, 7):
        text_copies[block, 0].wait_recv()
        hand_text(block)
    turn_texts(0)
    turn_texts(1)
    tiles((0, 0), (0, 1))
    wait_lines(1)
    wait_lines(2)
    tiles((1, 0), (1, 1), (2, 0), (2, 1))
    for block in (3, 5):
        text_copies[block, 0].wait_recv()
        hand_text(block)
    wait_lines(3)
    tiles((3, 0), (3, 1))
    for first in (0, HALF):
        text_copies[4, first].wait_recv()
    hand_text(4)
    turn_texts(3)
    tiles((3, 3), (1, 3), (2, 3), (0, 3))
    turn_texts(2)
    tiles((3, 2), (1, 2), (2, 2), (0, 2))

    lane_sums = [jnp.sum(sums[n], keepdims=True) for n in range(3)]
    found = jnp.where(row == 0, lane_sums[0], jnp.where(row == 1, lane_sums[1], lane_sums[2]))
    found_copies = spread(0, found, [twin])
    image_grads(3)
    send_lines(3, 0)
    send_lines(3, 1)
    text_grads(3)
    image_grads(1)
    send_lines(1, 0)
    found = collect(0, found, found_copies)
    found_copies = spread(1, found, list(column.values()))
    text_grads(2)
    text_sums(3)
    send_mid(3, 1, 0, ROWS, 0)
    send_mid(5, -1, 0, ROWS, 1)
    image_grads(2)
    send_lines(2, 0)
    send_lines(1, 1)
    send_lines(2, 1)
    text_sums(2)
    send_mid(4, 2, 0, HALF, 2)
    send_mid(4, -2, HALF, HALF, 3)
    text_grads(1)
    text_grads(0)
    image_grads(0)
    text_sums(1)
    send_share(7, 0)
    text_sums(0)
    send_share(1, 1)
    found = collect(1, found, found_copies)
    found_copies = spread(2, found, axes[1][1:])
    add_mid(2, 0, 2, 0, 2)
    add_mid(6, 1, 3, HALF, 3)

    for half in (0, 1):
        image_mid[half] = line_sum(half, 0).astype(jnp.bfloat16)
        for place in (3, 1, 2):
            back = AROUND_BACK[place]
            last_copies[half, back] = send(
                image_mid.at[half, pl.ds(place * HALF - HALF, HALF)], image_last.at[half, back],
                last_ss.at[half, place], last_rs.at[half, back], axes[half][place],
            )
    found = collect(2, found, found_copies)
    found_copies = spread(3, found, axes[0][1:])
    ends = [line_sum(half, 1) for half in (0, 1)]

    total = text_own[0:ROWS, :]
    for slot in range(4):
        gt_copies[slot].wait_recv()
        total = total + wide(text_in[slot])
    total_text_ref[...] = total

    for half in (0, 1):
        total = ends[half]
        for place in (1, 2, 3):
            last_copies[half, place].wait_recv()
            total = total + wide(image_last[half, place])
        rows = slice(half * HALF, half * HALF + HALF)
        total_image_ref[rows, :] = total

    found = collect(3, found, found_copies) * (1.0 / float(TOTAL) ** 2)
    lane = lax.broadcasted_iota(jnp.int32, (8, 128), 1)
    scale, slope = found[2:3] * temper[:, 0:128], found[1:2]
    scalars_ref[...] = jnp.where(row == 0, found, jnp.where(lane == 0, scale, slope))

    for copy in started:
        copy.wait_send()


def finish(image_ref, text_ref, total_image_ref, total_text_ref, scalars_ref, mean_ref, grad_image_ref, grad_text_ref, pair_ref):
    grad_image_ref[...] = back_rows(wide(image_ref[...]), total_image_ref[...])
    grad_text_ref[...] = back_rows(wide(text_ref[...]), total_text_ref[...])
    mean_ref[...] = scalars_ref[0, 0:1]
    pair_ref[...] = scalars_ref[1, 0:2]


def local(image_emb, text_emb, log_temp, bias):
    bf16, f32 = jnp.bfloat16, jnp.float32
    vmem, hbm = pl.BlockSpec(memory_space=pltpu.VMEM), pl.BlockSpec(memory_space=pltpu.HBM)
    dma = pltpu.SemaphoreType.DMA
    total_image, total_text, scalars = pl.pallas_call(
        kernel,
        out_shape=(
            jax.ShapeDtypeStruct((ROWS, WIDTH), f32),
            jax.ShapeDtypeStruct((ROWS, WIDTH), f32),
            jax.ShapeDtypeStruct((8, 128), f32),
        ),
        in_specs=[hbm] * 4,
        out_specs=(vmem, vmem, vmem),
        scratch_shapes=[
            pltpu.SMEM((1,), f32),
            pltpu.SMEM((1,), f32),
            pltpu.VMEM((ROWS, WIDTH), bf16),
            pltpu.VMEM((ROWS, WIDTH), bf16),
            pltpu.VMEM((16 * ROWS, WIDTH), bf16),
            pltpu.VMEM((16 * ROWS, WIDTH), bf16),
            pltpu.VMEM((WIDTH, 16 * ROWS), bf16),
            pltpu.VMEM((16 * ROWS, 16 * ROWS), bf16),
            pltpu.VMEM((16 * ROWS, 16 * ROWS), bf16),
            pltpu.VMEM((3, 8, 256), f32),
            pltpu.VMEM((16 * ROWS, WIDTH), bf16),
            pltpu.VMEM((GROUP, WIDTH), f32),
            pltpu.VMEM((2, 4, LINE, WIDTH), bf16),
            pltpu.VMEM((2, LINE - HALF, WIDTH), bf16),
            pltpu.VMEM((2, 4, HALF, WIDTH), bf16),
            pltpu.VMEM((8 * ROWS, WIDTH), bf16),
            pltpu.VMEM((8 * ROWS, WIDTH), f32),
            pltpu.VMEM((4, ROWS, WIDTH), bf16),
            pltpu.VMEM((8 * ROWS, WIDTH), bf16),
            pltpu.VMEM((8 * ROWS, WIDTH), bf16),
            pltpu.VMEM((4, ROWS, WIDTH), bf16),
            pltpu.VMEM((4, 7, 8, 128), f32),
            pltpu.VMEM((4, 8, 128), f32),
            dma((4,)),
            dma((2, 4, 4)), dma((2, 4, 4)), dma((8,)), dma((8,)), dma((8,)), dma((8,)),
            dma((2, 4, 2)), dma((2, 4, 2)), dma((2, 4)), dma((2, 4)),
            dma((4,)), dma((4,)), dma((4,)), dma((4,)), dma((4,)), dma((4,)),
            dma((4, 7)), dma((4, 7)),
        ],
        compiler_params=pltpu.CompilerParams(
            collective_id=0, has_side_effects=True, vmem_limit_bytes=56 * 1024 * 1024
        ),
    )(image_emb, text_emb, log_temp, bias)
    mean_loss, grad_image, grad_text, scalar_grads = pl.pallas_call(
        finish,
        out_shape=(
            jax.ShapeDtypeStruct((1,), f32),
            jax.ShapeDtypeStruct((ROWS, WIDTH), f32),
            jax.ShapeDtypeStruct((ROWS, WIDTH), f32),
            jax.ShapeDtypeStruct((2,), f32),
        ),
        in_specs=[vmem] * 5,
        out_specs=(vmem,) * 4,
    )(image_emb, text_emb, total_image, total_text, scalars)
    return (mean_loss, grad_image, grad_text, scalar_grads)


def solution(mesh):
    placed = (P(("blk", "narrow"), None), P(("blk", "narrow"), None), P(), P())
    return jax.shard_map(
        local,
        mesh=mesh,
        in_specs=placed,
        out_specs=(P(), P(("blk", "narrow"), None), P(("blk", "narrow"), None), P()),
        check_vma=False,
    )
```

```python
import math

import jax
import jax.numpy as jnp
from jax import lax
from jax.experimental import pallas as pl
from jax.experimental.pallas import tpu as pltpu
from jax.sharding import PartitionSpec as P

MESH = pl.DeviceIdType.MESH
ROWS, WIDTH = 64, 768
HALF, LINE, GROUP = ROWS // 2, 2 * ROWS, 4 * ROWS
TOTAL = 16384
LOG2E = math.log2(math.e)

AROUND = (0, 1, 3, 2)
AROUND_BACK = tuple(AROUND.index(-d % 4) for d in AROUND)
COLUMN = (0, 1, 7, 6, 2, 4, 3, 5)
COLUMN_BACK = tuple(COLUMN.index(-d % 8) for d in COLUMN)


def image_row(half, line, place):
    return line * GROUP + half * LINE + place * HALF


def text_row(other, place):
    return (place // 2 * 4 + other * 2 + place % 2) * ROWS


def row_scale(values):
    return lax.rsqrt(jnp.sum(values * values, axis=-1, keepdims=True) + 1e-06)


def back_rows(values, upstream):
    inverse = row_scale(values)
    unit = values * inverse
    return inverse * (upstream - unit * jnp.sum(unit * upstream, axis=-1, keepdims=True))


def fold(values):
    return jnp.sum(jnp.reshape(values, (values.shape[0] // 8, 8, values.shape[1])), axis=0)


def wide(ref):
    return ref.astype(jnp.float32)


def kernel(
    image_hbm, text_hbm, temp_hbm, bias_hbm,
    total_image_ref, total_text_ref, scalars_ref,
    temp_ref, bias_ref, image_ref, text_ref, images, texts, texts_t, slopes, slopes_t, sums,
    image_part, image_own, image_in, image_mid, image_last,
    text_part, text_own, text_in, pair_part, pair_in, text_mid, found_in, found_out,
    load, image_ss, image_rs, text_ss, text_rs, pair_ss, pair_rs,
    line_ss, line_rs, last_ss, last_rs, gt_ss, gt_rs, mid_ss, mid_rs, gp_ss, gp_rs, f_ss, f_rs,
):
    blk, narrow = lax.axis_index("blk"), lax.axis_index("narrow")
    x, core = lax.div(blk, 4), lax.rem(blk, 2)
    y = lax.rem(lax.div(blk, 2), 2) * 2 + lax.div(narrow, 8)
    z = lax.rem(narrow, 8)

    def device(dx, dy, dz, other):
        px, py, pz = lax.rem(x + dx, 4), lax.rem(y + dy, 4), lax.rem(z + dz, 8)
        pc = lax.rem(core + other, 2)
        return (px * 4 + lax.div(py, 2) * 2 + pc, lax.rem(py, 2) * 8 + pz)

    axes = ([device(d, 0, 0, 0) for d in AROUND], [device(0, d, 0, 0) for d in AROUND])
    column = {d: device(0, 0, d, 0) for d in range(1, 8)}
    twin = device(0, 0, 0, 1)

    barrier = pltpu.get_barrier_semaphore()
    peers = [axes[0][3], axes[1][3], *axes[0][1:3], *axes[1][1:3], *column.values(), twin]
    for peer in peers:
        pl.semaphore_signal(barrier, inc=1, device_id=peer, device_id_type=MESH)
    loads = [
        pltpu.make_async_copy(image_hbm, image_ref, load.at[0]),
        pltpu.make_async_copy(text_hbm, text_ref, load.at[1]),
        pltpu.make_async_copy(temp_hbm, temp_ref, load.at[2]),
        pltpu.make_async_copy(bias_hbm, bias_ref, load.at[3]),
    ]
    for copy in loads:
        copy.start()
    sums[...] = jnp.zeros_like(sums)
    for copy in loads:
        copy.wait()
    temper = jnp.exp(jnp.full((1, 256), temp_ref[0], jnp.float32))
    offset = jnp.full((1, 256), bias_ref[0], jnp.float32)
    temper2, offset2 = temper * LOG2E, offset * LOG2E
    temper3 = jnp.concatenate([temper] * 3, axis=1)
    image = wide(image_ref[...])
    image = (image * row_scale(image)).astype(jnp.bfloat16)
    for half in (0, 1):
        row = image_row(half, 0, 0)
        images[row : row + HALF, :] = image[half * HALF : half * HALF + HALF]
    text = wide(text_ref[...])
    texts[0:ROWS, :] = (text * row_scale(text)).astype(jnp.bfloat16)

    pl.semaphore_wait(barrier, len(peers))

    started = []

    def send(src, dst, send_sem, recv_sem, peer):
        copy = pltpu.make_async_remote_copy(
            src_ref=src, dst_ref=dst, send_sem=send_sem, recv_sem=recv_sem,
            device_id=peer, device_id_type=MESH,
        )
        copy.start()
        started.append(copy)
        return copy

    image_copies, text_copies, pair_copies = {}, {}, {}

    def first_image(half, place):
        back = AROUND_BACK[place]
        image_copies[half, 0, back] = send(
            images.at[pl.ds(image_row(half, 0, 0), HALF)],
            images.at[pl.ds(image_row(half, 0, back), HALF)],
            image_ss.at[half, 0, place], image_rs.at[half, 0, back], axes[half][place],
        )

    def pass_images(place):
        for line in (1, 2, 3):
            back = AROUND_BACK[line]
            for half in (0, 1):
                image_copies[half, back, place] = send(
                    images.at[pl.ds(image_row(half, 0, place), HALF)],
                    images.at[pl.ds(image_row(half, back, place), HALF)],
                    image_ss.at[half, line, place], image_rs.at[half, back, place], axes[1 - half][line],
                )

    def send_text(block, step, first, count, slot):
        source, target = text_row(0, COLUMN.index(block)), text_row(0, COLUMN.index((block - step) % 8))
        text_copies[(block - step) % 8, first] = send(
            texts.at[pl.ds(source + first, count)], texts.at[pl.ds(target + first, count)],
            text_ss.at[slot], text_rs.at[slot], column[step % 8],
        )

    def hand_text(block):
        place = COLUMN.index(block)
        pair_copies[block] = send(
            texts.at[pl.ds(text_row(0, place), ROWS)], texts.at[pl.ds(text_row(1, place), ROWS)],
            pair_ss.at[place], pair_rs.at[place], twin,
        )

    send_text(0, 2, HALF, HALF, 0)
    send_text(0, -2, 0, HALF, 1)
    for place in (1, 2, 3):
        for half in (0, 1):
            first_image(half, place)
    send_text(0, 2, 0, HALF, 2)
    send_text(0, -2, HALF, HALF, 3)
    hand_text(0)
    pass_images(0)
    send_text(0, 1, 0, ROWS, 4)
    send_text(0, -1, 0, ROWS, 5)
    for place in (1, 2, 3):
        for half in (0, 1):
            image_copies[half, 0, place].wait_recv()
        pass_images(place)
    text_copies[2, 0].wait_recv()
    send_text(2, -1, 0, HALF, 6)
    send_text(2, -2, 0, HALF, 7)
    text_copies[6, HALF].wait_recv()
    send_text(6, 1, HALF, HALF, 8)
    send_text(6, 2, HALF, HALF, 9)
    text_copies[2, HALF].wait_recv()
    send_text(2, -1, HALF, HALF, 10)
    text_copies[6, 0].wait_recv()
    send_text(6, 1, 0, HALF, 11)
    hand_text(2)
    hand_text(6)

    def pairs(products, first, second):
        rows = slice(first * GROUP, first * GROUP + GROUP)
        cols = slice(second * GROUP, second * GROUP + GROUP)
        grown = jnp.exp2(products * temper2 + offset2)
        above = 1.0 + grown
        slope = grown / above
        packed = above[0:128] * above[128:256]
        packed = packed[0:64] * packed[64:128]
        packed = packed[0:32] * packed[32:64]
        loss = fold(jnp.log(packed))
        if first == 0 and second == 0:
            row = lax.broadcasted_iota(jnp.int32, (GROUP, GROUP), 0)
            col = lax.broadcasted_iota(jnp.int32, (GROUP, GROUP), 1)
            upper = (row == col) & (row < HALF)
            lower = (row - LINE + HALF == col) & (row >= LINE) & (row < LINE + HALF)
            matched = jnp.where(upper | lower, 1.0, 0.0)
            slope = slope - matched
            loss = loss - fold(matched * (products * temper + offset))
        slope_b = slope.astype(jnp.bfloat16)
        slopes[rows, cols] = slope_b
        slopes_t[cols, rows] = slope_b.T
        return loss, fold(slope), fold(slope * products)

    def tiles(*places):
        products = [
            jnp.dot(
                images[first * GROUP : first * GROUP + GROUP, :],
                texts_t[:, second * GROUP : second * GROUP + GROUP],
                preferred_element_type=jnp.float32,
            )
            for first, second in places
        ]
        shares = [pairs(product, *place) for product, place in zip(products, places)]
        for n in range(3):
            sums[n] += sum(share[n] for share in shares)

    def wait_lines(line):
        for half in (0, 1):
            for place in range(4):
                image_copies[half, line, place].wait_recv()

    def turn_texts(group):
        for block in COLUMN[2 * group : 2 * group + 2]:
            pair_copies[block].wait_recv()
        rows = slice(group * GROUP, group * GROUP + GROUP)
        texts_t[:, rows] = texts[rows, :].T

    def spread(stage, values, peers):
        found_out[stage] = values
        return [
            send(found_out.at[stage], found_in.at[stage, n], f_ss.at[stage, n], f_rs.at[stage, n], peer)
            for n, peer in enumerate(peers)
        ]

    def collect(stage, values, copies):
        for n, copy in enumerate(copies):
            copy.wait_recv()
            values = values + found_in[stage, n]
        return values

    row = lax.broadcasted_iota(jnp.int32, (8, 128), 0)
    line_copies, last_copies, gt_copies, mid_copies, gp_copies = {}, {}, {}, {}, {}

    def image_grads(line):
        rows = slice(line * GROUP, line * GROUP + GROUP)
        part = temper3 * jnp.dot(slopes[rows, :], texts[...], preferred_element_type=jnp.float32)
        if line == 0:
            image_own[...] = part
        else:
            image_part[rows, :] = part.astype(jnp.bfloat16)

    def send_lines(line, own):
        first, count = (0, HALF) if own else (HALF, LINE - HALF)
        back = AROUND_BACK[line]
        for half in (0, 1):
            line_copies[half, back, own] = send(
                image_part.at[pl.ds(image_row(half, line, 0) + first, count)],
                image_in.at[half, back, pl.ds(first, count)],
                line_ss.at[half, line, own], line_rs.at[half, back, own], axes[1 - half][line],
            )

    def line_sum(half, own):
        first, count = (0, HALF) if own else (HALF, LINE - HALF)
        row = half * LINE + first
        part = image_own[row : row + count, :]
        for line in (3, 1, 2):
            line_copies[half, line, own].wait_recv()
            part = part + wide(image_in[half, line, first : first + count, :])
        return part

    def text_grads(group):
        rows = slice(group * GROUP, group * GROUP + GROUP)
        part = temper3 * jnp.dot(slopes_t[rows, :], images[...], preferred_element_type=jnp.float32)
        own = slice(group * LINE, group * LINE + LINE)
        text_own[own, :] = part[0:LINE]
        pair_part[own, :] = part[LINE:GROUP].astype(jnp.bfloat16)
        gp_copies[group] = send(
            pair_part.at[own], pair_in.at[own], gp_ss.at[group], gp_rs.at[group], twin
        )

    def own_rows(block, first=0, count=ROWS):
        place = COLUMN.index(block)
        return slice(place * ROWS + first, place * ROWS + first + count)

    def text_sums(group):
        gp_copies[group].wait_recv()
        own = slice(group * LINE, group * LINE + LINE)
        part = text_own[own, :] + wide(pair_in[own, :])
        text_own[own, :] = part
        text_part[own, :] = part.astype(jnp.bfloat16)

    def send_mid(block, step, first, count, slot):
        mid_copies[slot] = send(
            text_part.at[own_rows(block, first, count)], text_mid.at[slot, pl.ds(first, count)],
            mid_ss.at[slot], mid_rs.at[slot], column[step % 8],
        )

    def send_share(block, slot):
        gt_copies[slot] = send(
            text_part.at[own_rows(block)], text_in.at[slot], gt_ss.at[slot], gt_rs.at[slot], column[block]
        )

    def add_mid(block, near, far, first, slot):
        mid_copies[near].wait_recv()
        part = text_own[own_rows(block), :] + wide(text_mid[near])
        mid_copies[far].wait_recv()
        more = part[first : first + HALF] + wide(text_mid[far, first : first + HALF, :])
        part = jnp.concatenate([more, part[HALF:]] if first == 0 else [part[:HALF], more], axis=0)
        text_part[own_rows(block), :] = part.astype(jnp.bfloat16)
        send_share(block, slot)

    for block in (1, 7):
        text_copies[block, 0].wait_recv()
        hand_text(block)
    turn_texts(0)
    turn_texts(1)
    tiles((0, 0), (0, 1))
    wait_lines(1)
    wait_lines(2)
    tiles((1, 0), (1, 1), (2, 0), (2, 1))
    for block in (3, 5):
        for first in (0, HALF):
            text_copies[block, first].wait_recv()
        hand_text(block)
    wait_lines(3)
    tiles((3, 0), (3, 1))
    for first in (0, HALF):
        text_copies[4, first].wait_recv()
    hand_text(4)
    turn_texts(3)
    tiles((3, 3), (1, 3), (2, 3), (0, 3))
    turn_texts(2)
    tiles((3, 2), (1, 2), (2, 2), (0, 2))

    lane_sums = [jnp.sum(sums[n], keepdims=True) for n in range(3)]
    found = jnp.where(row == 0, lane_sums[0], jnp.where(row == 1, lane_sums[1], lane_sums[2]))
    found_copies = spread(0, found, [twin])
    image_grads(3)
    send_lines(3, 0)
    text_grads(3)
    image_grads(1)
    send_lines(1, 0)
    found = collect(0, found, found_copies)
    found_copies = spread(1, found, list(column.values()))
    text_grads(2)
    text_sums(3)
    send_mid(3, 1, 0, ROWS, 0)
    send_mid(5, -1, 0, ROWS, 1)
    image_grads(2)
    send_lines(2, 0)
    for line in (3, 1, 2):
        send_lines(line, 1)
    text_sums(2)
    send_mid(4, 2, 0, HALF, 2)
    send_mid(4, -2, HALF, HALF, 3)
    text_grads(1)
    text_grads(0)
    image_grads(0)
    text_sums(1)
    send_share(7, 0)
    text_sums(0)
    send_share(1, 1)
    found = collect(1, found, found_copies)
    found_copies = spread(2, found, axes[1][1:])
    add_mid(2, 0, 2, 0, 2)
    add_mid(6, 1, 3, HALF, 3)

    for half in (0, 1):
        image_mid[half] = line_sum(half, 0).astype(jnp.bfloat16)
        for place in (3, 1, 2):
            back = AROUND_BACK[place]
            last_copies[half, back] = send(
                image_mid.at[half, pl.ds(place * HALF - HALF, HALF)], image_last.at[half, back],
                last_ss.at[half, place], last_rs.at[half, back], axes[half][place],
            )
    found = collect(2, found, found_copies)
    found_copies = spread(3, found, axes[0][1:])
    ends = [line_sum(half, 1) for half in (0, 1)]

    total = text_own[0:ROWS, :]
    for slot in range(4):
        gt_copies[slot].wait_recv()
        total = total + wide(text_in[slot])
    total_text_ref[...] = total

    for half in (0, 1):
        total = ends[half]
        for place in (1, 2, 3):
            last_copies[half, place].wait_recv()
            total = total + wide(image_last[half, place])
        rows = slice(half * HALF, half * HALF + HALF)
        total_image_ref[rows, :] = total

    found = collect(3, found, found_copies) * (1.0 / float(TOTAL) ** 2)
    lane = lax.broadcasted_iota(jnp.int32, (8, 128), 1)
    scale, slope = found[2:3] * temper[:, 0:128], found[1:2]
    scalars_ref[...] = jnp.where(row == 0, found, jnp.where(lane == 0, scale, slope))

    for copy in started:
        copy.wait_send()


def finish(image_ref, text_ref, total_image_ref, total_text_ref, scalars_ref, mean_ref, grad_image_ref, grad_text_ref, pair_ref):
    grad_image_ref[...] = back_rows(wide(image_ref[...]), total_image_ref[...])
    grad_text_ref[...] = back_rows(wide(text_ref[...]), total_text_ref[...])
    mean_ref[...] = scalars_ref[0, 0:1]
    pair_ref[...] = scalars_ref[1, 0:2]


def local(image_emb, text_emb, log_temp, bias):
    bf16, f32 = jnp.bfloat16, jnp.float32
    vmem, hbm = pl.BlockSpec(memory_space=pltpu.VMEM), pl.BlockSpec(memory_space=pltpu.HBM)
    dma = pltpu.SemaphoreType.DMA
    total_image, total_text, scalars = pl.pallas_call(
        kernel,
        out_shape=(
            jax.ShapeDtypeStruct((ROWS, WIDTH), f32),
            jax.ShapeDtypeStruct((ROWS, WIDTH), f32),
            jax.ShapeDtypeStruct((8, 128), f32),
        ),
        in_specs=[hbm] * 4,
        out_specs=(vmem, vmem, vmem),
        scratch_shapes=[
            pltpu.SMEM((1,), f32),
            pltpu.SMEM((1,), f32),
            pltpu.VMEM((ROWS, WIDTH), bf16),
            pltpu.VMEM((ROWS, WIDTH), bf16),
            pltpu.VMEM((16 * ROWS, WIDTH), bf16),
            pltpu.VMEM((16 * ROWS, WIDTH), bf16),
            pltpu.VMEM((WIDTH, 16 * ROWS), bf16),
            pltpu.VMEM((16 * ROWS, 16 * ROWS), bf16),
            pltpu.VMEM((16 * ROWS, 16 * ROWS), bf16),
            pltpu.VMEM((3, 8, 256), f32),
            pltpu.VMEM((16 * ROWS, WIDTH), bf16),
            pltpu.VMEM((GROUP, WIDTH), f32),
            pltpu.VMEM((2, 4, LINE, WIDTH), bf16),
            pltpu.VMEM((2, LINE - HALF, WIDTH), bf16),
            pltpu.VMEM((2, 4, HALF, WIDTH), bf16),
            pltpu.VMEM((8 * ROWS, WIDTH), bf16),
            pltpu.VMEM((8 * ROWS, WIDTH), f32),
            pltpu.VMEM((4, ROWS, WIDTH), bf16),
            pltpu.VMEM((8 * ROWS, WIDTH), bf16),
            pltpu.VMEM((8 * ROWS, WIDTH), bf16),
            pltpu.VMEM((4, ROWS, WIDTH), bf16),
            pltpu.VMEM((4, 7, 8, 128), f32),
            pltpu.VMEM((4, 8, 128), f32),
            dma((4,)),
            dma((2, 4, 4)), dma((2, 4, 4)), dma((12,)), dma((12,)), dma((8,)), dma((8,)),
            dma((2, 4, 2)), dma((2, 4, 2)), dma((2, 4)), dma((2, 4)),
            dma((4,)), dma((4,)), dma((4,)), dma((4,)), dma((4,)), dma((4,)),
            dma((4, 7)), dma((4, 7)),
        ],
        compiler_params=pltpu.CompilerParams(
            collective_id=0, has_side_effects=True, vmem_limit_bytes=56 * 1024 * 1024
        ),
    )(image_emb, text_emb, log_temp, bias)
    mean_loss, grad_image, grad_text, scalar_grads = pl.pallas_call(
        finish,
        out_shape=(
            jax.ShapeDtypeStruct((1,), f32),
            jax.ShapeDtypeStruct((ROWS, WIDTH), f32),
            jax.ShapeDtypeStruct((ROWS, WIDTH), f32),
            jax.ShapeDtypeStruct((2,), f32),
        ),
        in_specs=[vmem] * 5,
        out_specs=(vmem,) * 4,
    )(image_emb, text_emb, total_image, total_text, scalars)
    return (mean_loss, grad_image, grad_text, scalar_grads)


def solution(mesh):
    placed = (P(("blk", "narrow"), None), P(("blk", "narrow"), None), P(), P())
    return jax.shard_map(
        local,
        mesh=mesh,
        in_specs=placed,
        out_specs=(P(), P(("blk", "narrow"), None), P(("blk", "narrow"), None), P()),
        check_vma=False,
    )
```

```python
import math

import jax
import jax.numpy as jnp
from jax import lax
from jax.experimental import pallas as pl
from jax.experimental.pallas import tpu as pltpu
from jax.sharding import PartitionSpec as P

MESH = pl.DeviceIdType.MESH
ROWS, WIDTH = 64, 768
HALF, LINE, GROUP = ROWS // 2, 2 * ROWS, 4 * ROWS
TOTAL = 16384
LOG2E = math.log2(math.e)

AROUND = (0, 1, 3, 2)
AROUND_BACK = tuple(AROUND.index(-d % 4) for d in AROUND)
COLUMN = (0, 1, 7, 6, 2, 4, 3, 5)
FOUND = (0, 1, 8, 11, 14)
COLUMN_BACK = tuple(COLUMN.index(-d % 8) for d in COLUMN)


def image_row(half, line, place):
    return line * GROUP + half * LINE + place * HALF


def text_row(other, place):
    return (place // 2 * 4 + other * 2 + place % 2) * ROWS


def row_scale(values):
    return lax.rsqrt(jnp.sum(values * values, axis=-1, keepdims=True) + 1e-06)


def back_rows(values, upstream):
    inverse = row_scale(values)
    unit = values * inverse
    return inverse * (upstream - unit * jnp.sum(unit * upstream, axis=-1, keepdims=True))


def fold(values):
    return jnp.sum(jnp.reshape(values, (values.shape[0] // 8, 8, values.shape[1])), axis=0)


def wide(ref):
    return ref.astype(jnp.float32)


def kernel(
    image_hbm, text_hbm, temp_hbm, bias_hbm,
    total_image_ref, total_text_ref, scalars_ref,
    temp_ref, bias_ref, image_ref, text_ref, images, texts, texts_t, slopes, slopes_t, sums,
    image_part, image_own, image_in, image_mid, image_last,
    text_part, text_own, text_in, pair_part, pair_in, text_mid, found_in, found_out,
    load, image_ss, image_rs, lines_rs, text_ss, text_rs, pair_ss, pair_rs,
    line_ss, line_rs, last_ss, last_rs, gt_ss, gt_rs, mid_ss, mid_rs, gp_ss, gp_rs, f_ss, f_rs,
):
    blk, narrow = lax.axis_index("blk"), lax.axis_index("narrow")
    x, core = lax.div(blk, 4), lax.rem(blk, 2)
    y = lax.rem(lax.div(blk, 2), 2) * 2 + lax.div(narrow, 8)
    z = lax.rem(narrow, 8)

    def device(dx, dy, dz, other):
        px, py, pz = lax.rem(x + dx, 4), lax.rem(y + dy, 4), lax.rem(z + dz, 8)
        pc = lax.rem(core + other, 2)
        return (px * 4 + lax.div(py, 2) * 2 + pc, lax.rem(py, 2) * 8 + pz)

    axes = ([device(d, 0, 0, 0) for d in AROUND], [device(0, d, 0, 0) for d in AROUND])
    column = {d: device(0, 0, d, 0) for d in range(1, 8)}
    twin = device(0, 0, 0, 1)

    barrier = pltpu.get_barrier_semaphore()
    peers = [axes[0][3], axes[1][3], *axes[0][1:3], *axes[1][1:3], *column.values(), twin]
    for peer in peers:
        pl.semaphore_signal(barrier, inc=1, device_id=peer, device_id_type=MESH)
    loads = [
        pltpu.make_async_copy(image_hbm, image_ref, load.at[0]),
        pltpu.make_async_copy(text_hbm, text_ref, load.at[1]),
        pltpu.make_async_copy(temp_hbm, temp_ref, load.at[2]),
        pltpu.make_async_copy(bias_hbm, bias_ref, load.at[3]),
    ]
    for copy in loads:
        copy.start()
    sums[...] = jnp.zeros_like(sums)
    for copy in loads:
        copy.wait()
    temper = jnp.exp(jnp.full((1, 256), temp_ref[0], jnp.float32))
    offset = jnp.full((1, 256), bias_ref[0], jnp.float32)
    temper2, offset2 = temper * LOG2E, offset * LOG2E
    temper3 = jnp.concatenate([temper] * 3, axis=1)
    image = wide(image_ref[...])
    image = (image * row_scale(image)).astype(jnp.bfloat16)
    for half in (0, 1):
        row = image_row(half, 0, 0)
        images[row : row + HALF, :] = image[half * HALF : half * HALF + HALF]
    text = wide(text_ref[...])
    texts[0:ROWS, :] = (text * row_scale(text)).astype(jnp.bfloat16)

    pl.semaphore_wait(barrier, len(peers))


    def send(src, dst, send_sem, recv_sem, peer):
        copy = pltpu.make_async_remote_copy(
            src_ref=src, dst_ref=dst, send_sem=send_sem, recv_sem=recv_sem,
            device_id=peer, device_id_type=MESH,
        )
        copy.start()
        return copy

    def wait_bytes(ref, sem):
        pltpu.make_async_copy(ref, ref, sem).wait()

    image_copies, text_copies, pair_copies = {}, {}, {}

    def first_image(half, place):
        back = AROUND_BACK[place]
        image_copies[half, 0, back] = send(
            images.at[pl.ds(image_row(half, 0, 0), HALF)],
            images.at[pl.ds(image_row(half, 0, back), HALF)],
            image_ss.at[0], image_rs.at[half, back], axes[half][place],
        )

    def pass_images(place):
        for line in (1, 2, 3):
            back = AROUND_BACK[line]
            for half in (0, 1):
                image_copies[half, back, place] = send(
                    images.at[pl.ds(image_row(half, 0, place), HALF)],
                    images.at[pl.ds(image_row(half, back, place), HALF)],
                    image_ss.at[0], lines_rs.at[back], axes[1 - half][line],
                )

    def send_text(block, step, first, count, slot):
        source, target = text_row(0, COLUMN.index(block)), text_row(0, COLUMN.index((block - step) % 8))
        text_copies[(block - step) % 8, first] = send(
            texts.at[pl.ds(source + first, count)], texts.at[pl.ds(target + first, count)],
            text_ss.at[0], text_rs.at[slot], column[step % 8],
        )

    def hand_text(block):
        place = COLUMN.index(block)
        pair_copies[block] = send(
            texts.at[pl.ds(text_row(0, place), ROWS)], texts.at[pl.ds(text_row(1, place), ROWS)],
            pair_ss.at[0], pair_rs.at[place], twin,
        )

    send_text(0, 2, HALF, HALF, 0)
    send_text(0, -2, 0, HALF, 1)
    for place in (1, 2, 3):
        for half in (0, 1):
            first_image(half, place)
    send_text(0, 2, 0, HALF, 2)
    send_text(0, -2, HALF, HALF, 3)
    hand_text(0)
    pass_images(0)
    send_text(0, 1, 0, ROWS, 4)
    send_text(0, -1, 0, ROWS, 5)
    for place in (1, 2, 3):
        for half in (0, 1):
            image_copies[half, 0, place].wait_recv()
        pass_images(place)
    text_copies[2, 0].wait_recv()
    send_text(2, -1, 0, HALF, 6)
    send_text(2, -2, 0, HALF, 7)
    text_copies[6, HALF].wait_recv()
    send_text(6, 1, HALF, HALF, 8)
    send_text(6, 2, HALF, HALF, 9)
    text_copies[2, HALF].wait_recv()
    send_text(2, -1, HALF, HALF, 10)
    text_copies[6, 0].wait_recv()
    send_text(6, 1, 0, HALF, 11)
    hand_text(2)
    hand_text(6)

    def pairs(products, first, second):
        rows = slice(first * GROUP, first * GROUP + GROUP)
        cols = slice(second * GROUP, second * GROUP + GROUP)
        grown = jnp.exp2(products * temper2 + offset2)
        above = 1.0 + grown
        slope = grown / above
        packed = above[0:128] * above[128:256]
        packed = packed[0:64] * packed[64:128]
        packed = packed[0:32] * packed[32:64]
        loss = fold(jnp.log(packed))
        if first == 0 and second == 0:
            row = lax.broadcasted_iota(jnp.int32, (GROUP, GROUP), 0)
            col = lax.broadcasted_iota(jnp.int32, (GROUP, GROUP), 1)
            upper = (row == col) & (row < HALF)
            lower = (row - LINE + HALF == col) & (row >= LINE) & (row < LINE + HALF)
            matched = jnp.where(upper | lower, 1.0, 0.0)
            slope = slope - matched
            loss = loss - fold(matched * (products * temper + offset))
        slope_b = slope.astype(jnp.bfloat16)
        slopes[rows, cols] = slope_b
        slopes_t[cols, rows] = slope_b.T
        return loss, fold(slope), fold(slope * products)

    def tiles(*places):
        products = [
            jnp.dot(
                images[first * GROUP : first * GROUP + GROUP, :],
                texts_t[:, second * GROUP : second * GROUP + GROUP],
                preferred_element_type=jnp.float32,
            )
            for first, second in places
        ]
        shares = [pairs(product, *place) for product, place in zip(products, places)]
        for n in range(3):
            sums[n] += sum(share[n] for share in shares)

    def wait_lines(line):
        wait_bytes(images.at[pl.ds(line * GROUP, GROUP)], lines_rs.at[line])

    def turn_texts(group):
        for block in COLUMN[2 * group : 2 * group + 2]:
            pair_copies[block].wait_recv()
        rows = slice(group * GROUP, group * GROUP + GROUP)
        texts_t[:, rows] = texts[rows, :].T

    def spread(stage, values, peers):
        found_out[stage] = values
        first = FOUND[stage]
        for n, peer in enumerate(peers):
            send(found_out.at[stage], found_in.at[first + n], f_ss.at[0], f_rs.at[stage], peer)

    def collect(stage, values):
        first, end = FOUND[stage], FOUND[stage + 1]
        wait_bytes(found_in.at[pl.ds(first, end - first)], f_rs.at[stage])
        for n in range(first, end):
            values = values + found_in[n]
        return values

    row = lax.broadcasted_iota(jnp.int32, (8, 128), 0)
    mid_copies, gp_copies = {}, {}

    def image_grads(line):
        rows = slice(line * GROUP, line * GROUP + GROUP)
        part = temper3 * jnp.dot(slopes[rows, :], texts[...], preferred_element_type=jnp.float32)
        if line == 0:
            image_own[...] = part
        else:
            image_part[rows, :] = part.astype(jnp.bfloat16)

    def send_lines(line, own):
        first, count = (0, HALF) if own else (HALF, LINE - HALF)
        back = AROUND_BACK[line]
        for half in (0, 1):
            send(
                image_part.at[pl.ds(image_row(half, line, 0) + first, count)],
                image_in.at[half, back, pl.ds(first, count)],
                line_ss.at[0], line_rs.at[half, own], axes[1 - half][line],
            )

    def line_sum(half, own):
        first, count = (0, HALF) if own else (HALF, LINE - HALF)
        row = half * LINE + first
        part = image_own[row : row + count, :]
        wait_bytes(image_in.at[half, pl.ds(1, 3), pl.ds(first, count)], line_rs.at[half, own])
        for line in (3, 1, 2):
            part = part + wide(image_in[half, line, first : first + count, :])
        return part

    def text_grads(group):
        rows = slice(group * GROUP, group * GROUP + GROUP)
        part = temper3 * jnp.dot(slopes_t[rows, :], images[...], preferred_element_type=jnp.float32)
        own = slice(group * LINE, group * LINE + LINE)
        text_own[own, :] = part[0:LINE]
        pair_part[own, :] = part[LINE:GROUP].astype(jnp.bfloat16)
        gp_copies[group] = send(
            pair_part.at[own], pair_in.at[own], gp_ss.at[0], gp_rs.at[group], twin
        )

    def own_rows(block, first=0, count=ROWS):
        place = COLUMN.index(block)
        return slice(place * ROWS + first, place * ROWS + first + count)

    def text_sums(group):
        gp_copies[group].wait_recv()
        own = slice(group * LINE, group * LINE + LINE)
        part = text_own[own, :] + wide(pair_in[own, :])
        text_own[own, :] = part
        text_part[own, :] = part.astype(jnp.bfloat16)

    def send_mid(block, step, first, count, slot):
        mid_copies[slot] = send(
            text_part.at[own_rows(block, first, count)], text_mid.at[slot, pl.ds(first, count)],
            mid_ss.at[0], mid_rs.at[slot], column[step % 8],
        )

    def send_share(block, slot):
        send(
            text_part.at[own_rows(block)], text_in.at[slot], gt_ss.at[0], gt_rs.at[0], column[block]
        )

    def add_mid(block, near, far, first, slot):
        mid_copies[near].wait_recv()
        part = text_own[own_rows(block), :] + wide(text_mid[near])
        mid_copies[far].wait_recv()
        more = part[first : first + HALF] + wide(text_mid[far, first : first + HALF, :])
        part = jnp.concatenate([more, part[HALF:]] if first == 0 else [part[:HALF], more], axis=0)
        text_part[own_rows(block), :] = part.astype(jnp.bfloat16)
        send_share(block, slot)

    for block in (1, 7):
        text_copies[block, 0].wait_recv()
        hand_text(block)
    turn_texts(0)
    turn_texts(1)
    tiles((0, 0), (0, 1))
    wait_lines(1)
    wait_lines(2)
    tiles((1, 0), (1, 1), (2, 0), (2, 1))
    for block in (3, 5):
        for first in (0, HALF):
            text_copies[block, first].wait_recv()
        hand_text(block)
    wait_lines(3)
    tiles((3, 0), (3, 1))
    for first in (0, HALF):
        text_copies[4, first].wait_recv()
    hand_text(4)
    turn_texts(3)
    tiles((3, 3), (1, 3), (2, 3), (0, 3))
    turn_texts(2)
    tiles((3, 2), (1, 2), (2, 2), (0, 2))

    lane_sums = [jnp.sum(sums[n], keepdims=True) for n in range(3)]
    found = jnp.where(row == 0, lane_sums[0], jnp.where(row == 1, lane_sums[1], lane_sums[2]))
    spread(0, found, [twin])
    image_grads(3)
    send_lines(3, 0)
    text_grads(3)
    image_grads(1)
    send_lines(1, 0)
    found = collect(0, found)
    spread(1, found, list(column.values()))
    text_grads(2)
    text_sums(3)
    send_mid(3, 1, 0, ROWS, 0)
    send_mid(5, -1, 0, ROWS, 1)
    image_grads(2)
    send_lines(2, 0)
    for line in (3, 1, 2):
        send_lines(line, 1)
    text_sums(2)
    send_mid(4, 2, 0, HALF, 2)
    send_mid(4, -2, HALF, HALF, 3)
    text_grads(1)
    text_grads(0)
    image_grads(0)
    text_sums(1)
    send_share(7, 0)
    text_sums(0)
    send_share(1, 1)
    found = collect(1, found)
    spread(2, found, axes[1][1:])
    add_mid(2, 0, 2, 0, 2)
    add_mid(6, 1, 3, HALF, 3)

    for half in (0, 1):
        image_mid[half] = line_sum(half, 0).astype(jnp.bfloat16)
        for place in (3, 1, 2):
            back = AROUND_BACK[place]
            send(
                image_mid.at[half, pl.ds(place * HALF - HALF, HALF)], image_last.at[half, back],
                last_ss.at[0], last_rs.at[half], axes[half][place],
            )
    found = collect(2, found)
    spread(3, found, axes[0][1:])
    ends = [line_sum(half, 1) for half in (0, 1)]

    total = text_own[0:ROWS, :]
    wait_bytes(text_in, gt_rs.at[0])
    for slot in range(4):
        total = total + wide(text_in[slot])
    total_text_ref[...] = total

    for half in (0, 1):
        total = ends[half]
        wait_bytes(image_last.at[half, pl.ds(1, 3)], last_rs.at[half])
        for place in (1, 2, 3):
            total = total + wide(image_last[half, place])
        rows = slice(half * HALF, half * HALF + HALF)
        total_image_ref[rows, :] = total

    found = collect(3, found) * (1.0 / float(TOTAL) ** 2)
    lane = lax.broadcasted_iota(jnp.int32, (8, 128), 1)
    scale, slope = found[2:3] * temper[:, 0:128], found[1:2]
    scalars_ref[...] = jnp.where(row == 0, found, jnp.where(lane == 0, scale, slope))

    wait_bytes(images.at[0 : 30 * HALF], image_ss.at[0])
    wait_bytes(texts.at[0 : 7 * ROWS], text_ss.at[0])
    wait_bytes(texts.at[0 : 8 * ROWS], pair_ss.at[0])
    wait_bytes(image_part.at[0 : 6 * LINE], line_ss.at[0])
    wait_bytes(image_mid, last_ss.at[0])
    wait_bytes(text_part.at[0 : 4 * ROWS], gt_ss.at[0])
    wait_bytes(text_part.at[0 : 3 * ROWS], mid_ss.at[0])
    wait_bytes(pair_part, gp_ss.at[0])
    wait_bytes(found_in.at[0 : FOUND[4]], f_ss.at[0])


def finish(image_ref, text_ref, total_image_ref, total_text_ref, scalars_ref, mean_ref, grad_image_ref, grad_text_ref, pair_ref):
    grad_image_ref[...] = back_rows(wide(image_ref[...]), total_image_ref[...])
    grad_text_ref[...] = back_rows(wide(text_ref[...]), total_text_ref[...])
    mean_ref[...] = scalars_ref[0, 0:1]
    pair_ref[...] = scalars_ref[1, 0:2]


def local(image_emb, text_emb, log_temp, bias):
    bf16, f32 = jnp.bfloat16, jnp.float32
    vmem, hbm = pl.BlockSpec(memory_space=pltpu.VMEM), pl.BlockSpec(memory_space=pltpu.HBM)
    dma = pltpu.SemaphoreType.DMA
    total_image, total_text, scalars = pl.pallas_call(
        kernel,
        out_shape=(
            jax.ShapeDtypeStruct((ROWS, WIDTH), f32),
            jax.ShapeDtypeStruct((ROWS, WIDTH), f32),
            jax.ShapeDtypeStruct((8, 128), f32),
        ),
        in_specs=[hbm] * 4,
        out_specs=(vmem, vmem, vmem),
        scratch_shapes=[
            pltpu.SMEM((1,), f32),
            pltpu.SMEM((1,), f32),
            pltpu.VMEM((ROWS, WIDTH), bf16),
            pltpu.VMEM((ROWS, WIDTH), bf16),
            pltpu.VMEM((16 * ROWS, WIDTH), bf16),
            pltpu.VMEM((16 * ROWS, WIDTH), bf16),
            pltpu.VMEM((WIDTH, 16 * ROWS), bf16),
            pltpu.VMEM((16 * ROWS, 16 * ROWS), bf16),
            pltpu.VMEM((16 * ROWS, 16 * ROWS), bf16),
            pltpu.VMEM((3, 8, 256), f32),
            pltpu.VMEM((16 * ROWS, WIDTH), bf16),
            pltpu.VMEM((GROUP, WIDTH), f32),
            pltpu.VMEM((2, 4, LINE, WIDTH), bf16),
            pltpu.VMEM((2, LINE - HALF, WIDTH), bf16),
            pltpu.VMEM((2, 4, HALF, WIDTH), bf16),
            pltpu.VMEM((8 * ROWS, WIDTH), bf16),
            pltpu.VMEM((8 * ROWS, WIDTH), f32),
            pltpu.VMEM((4, ROWS, WIDTH), bf16),
            pltpu.VMEM((8 * ROWS, WIDTH), bf16),
            pltpu.VMEM((8 * ROWS, WIDTH), bf16),
            pltpu.VMEM((4, ROWS, WIDTH), bf16),
            pltpu.VMEM((14, 8, 128), f32),
            pltpu.VMEM((4, 8, 128), f32),
            dma((4,)),
            dma((1,)), dma((2, 4)), dma((4,)), dma((1,)), dma((12,)), dma((1,)), dma((8,)),
            dma((1,)), dma((2, 2)), dma((1,)), dma((2,)), dma((1,)), dma((1,)),
            dma((1,)), dma((4,)), dma((1,)), dma((4,)), dma((1,)), dma((4,)),
        ],
        compiler_params=pltpu.CompilerParams(
            collective_id=0, has_side_effects=True, vmem_limit_bytes=56 * 1024 * 1024
        ),
    )(image_emb, text_emb, log_temp, bias)
    mean_loss, grad_image, grad_text, scalar_grads = pl.pallas_call(
        finish,
        out_shape=(
            jax.ShapeDtypeStruct((1,), f32),
            jax.ShapeDtypeStruct((ROWS, WIDTH), f32),
            jax.ShapeDtypeStruct((ROWS, WIDTH), f32),
            jax.ShapeDtypeStruct((2,), f32),
        ),
        in_specs=[vmem] * 5,
        out_specs=(vmem,) * 4,
    )(image_emb, text_emb, total_image, total_text, scalars)
    return (mean_loss, grad_image, grad_text, scalar_grads)


def solution(mesh):
    placed = (P(("blk", "narrow"), None), P(("blk", "narrow"), None), P(), P())
    return jax.shard_map(
        local,
        mesh=mesh,
        in_specs=placed,
        out_specs=(P(), P(("blk", "narrow"), None), P(("blk", "narrow"), None), P()),
        check_vma=False,
    )
```

```python
import math

import jax
import jax.numpy as jnp
from jax import lax
from jax.experimental import pallas as pl
from jax.experimental.pallas import tpu as pltpu
from jax.sharding import PartitionSpec as P

MESH = pl.DeviceIdType.MESH
ROWS, WIDTH = 64, 768
HALF, LINE, GROUP = ROWS // 2, 2 * ROWS, 4 * ROWS
TOTAL = 16384
LOG2E = math.log2(math.e)

AROUND = (0, 1, 3, 2)
AROUND_BACK = tuple(AROUND.index(-d % 4) for d in AROUND)
COLUMN = (0, 1, 7, 6, 2, 4, 3, 5)
FOUND = (0, 1, 8, 11, 14)
COLUMN_BACK = tuple(COLUMN.index(-d % 8) for d in COLUMN)


def image_row(half, line, place):
    return line * GROUP + half * LINE + place * HALF


def text_row(other, place):
    return (place // 2 * 4 + other * 2 + place % 2) * ROWS


def row_scale(values):
    return lax.rsqrt(jnp.sum(values * values, axis=-1, keepdims=True) + 1e-06)


def back_rows(values, upstream):
    inverse = row_scale(values)
    unit = values * inverse
    return inverse * (upstream - unit * jnp.sum(unit * upstream, axis=-1, keepdims=True))


def fold(values):
    return jnp.sum(jnp.reshape(values, (values.shape[0] // 8, 8, values.shape[1])), axis=0)


def wide(ref):
    return ref.astype(jnp.float32)


def kernel(
    image_hbm, text_hbm, temp_hbm, bias_hbm,
    total_image_ref, total_text_ref, scalars_ref,
    temp_ref, bias_ref, image_ref, text_ref, images, texts, texts_t, slopes, slopes_t, sums,
    image_part, image_own, image_in, image_mid, image_last,
    text_part, text_own, text_in, pair_part, pair_in, text_mid, found_in, found_out,
    load, image_ss, image_rs, lines_rs, text_ss, text_rs, pair_ss, pair_rs,
    line_ss, line_rs, last_ss, last_rs, gt_ss, gt_rs, mid_ss, mid_rs, gp_ss, gp_rs, f_ss, f_rs,
):
    blk, narrow = lax.axis_index("blk"), lax.axis_index("narrow")
    x, core = lax.div(blk, 4), lax.rem(blk, 2)
    y = lax.rem(lax.div(blk, 2), 2) * 2 + lax.div(narrow, 8)
    z = lax.rem(narrow, 8)

    def device(dx, dy, dz, other):
        px, py, pz = lax.rem(x + dx, 4), lax.rem(y + dy, 4), lax.rem(z + dz, 8)
        pc = lax.rem(core + other, 2)
        return (px * 4 + lax.div(py, 2) * 2 + pc, lax.rem(py, 2) * 8 + pz)

    axes = ([device(d, 0, 0, 0) for d in AROUND], [device(0, d, 0, 0) for d in AROUND])
    column = {d: device(0, 0, d, 0) for d in range(1, 8)}
    twin = device(0, 0, 0, 1)

    loads = [
        pltpu.make_async_copy(image_hbm, image_ref, load.at[0]),
        pltpu.make_async_copy(text_hbm, text_ref, load.at[1]),
        pltpu.make_async_copy(temp_hbm, temp_ref, load.at[2]),
        pltpu.make_async_copy(bias_hbm, bias_ref, load.at[3]),
    ]
    for copy in loads:
        copy.start()
    barrier = pltpu.get_barrier_semaphore()
    peers = [axes[0][3], axes[1][3], *axes[0][1:3], *axes[1][1:3], *column.values(), twin]
    for peer in peers:
        pl.semaphore_signal(barrier, inc=1, device_id=peer, device_id_type=MESH)

    loads[0].wait()
    image = wide(image_ref[...])
    image = (image * row_scale(image)).astype(jnp.bfloat16)
    for half in (0, 1):
        row = image_row(half, 0, 0)
        images[row : row + HALF, :] = image[half * HALF : half * HALF + HALF]

    pl.semaphore_wait(barrier, len(peers))

    def send(src, dst, send_sem, recv_sem, peer):
        copy = pltpu.make_async_remote_copy(
            src_ref=src, dst_ref=dst, send_sem=send_sem, recv_sem=recv_sem,
            device_id=peer, device_id_type=MESH,
        )
        copy.start()
        return copy

    def wait_bytes(ref, sem):
        pltpu.make_async_copy(ref, ref, sem).wait()

    text_copies = {}

    def first_image(half, place):
        back = AROUND_BACK[place]
        send(
            images.at[pl.ds(image_row(half, 0, 0), HALF)],
            images.at[pl.ds(image_row(half, 0, back), HALF)],
            image_ss.at[0], image_rs.at[back], axes[half][place],
        )

    def pass_images(place):
        for line in (1, 2, 3):
            back = AROUND_BACK[line]
            for half in (0, 1):
                send(
                    images.at[pl.ds(image_row(half, 0, place), HALF)],
                    images.at[pl.ds(image_row(half, back, place), HALF)],
                    image_ss.at[0], lines_rs.at[back], axes[1 - half][line],
                )

    def send_text(block, step, first, count, slot):
        source, target = text_row(0, COLUMN.index(block)), text_row(0, COLUMN.index((block - step) % 8))
        text_copies[(block - step) % 8, first] = send(
            texts.at[pl.ds(source + first, count)], texts.at[pl.ds(target + first, count)],
            text_ss.at[0], text_rs.at[slot], column[step % 8],
        )

    def hand_text(block):
        place = COLUMN.index(block)
        send(
            texts.at[pl.ds(text_row(0, place), ROWS)], texts.at[pl.ds(text_row(1, place), ROWS)],
            pair_ss.at[0], pair_rs.at[place // 2], twin,
        )

    for place in (1, 2, 3):
        for half in (0, 1):
            first_image(half, place)
    loads[1].wait()
    text = wide(text_ref[...])
    texts[0:ROWS, :] = (text * row_scale(text)).astype(jnp.bfloat16)
    send_text(0, 2, HALF, HALF, 0)
    send_text(0, -2, 0, HALF, 1)
    send_text(0, 2, 0, HALF, 2)
    send_text(0, -2, HALF, HALF, 3)
    hand_text(0)
    pass_images(0)
    send_text(0, 1, 0, ROWS, 4)
    send_text(0, -1, 0, ROWS, 5)

    for copy in loads[2:]:
        copy.wait()
    temper = jnp.exp(jnp.full((1, 256), temp_ref[0], jnp.float32))
    offset = jnp.full((1, 256), bias_ref[0], jnp.float32)
    temper2, offset2 = temper * LOG2E, offset * LOG2E
    temper3 = jnp.concatenate([temper] * 3, axis=1)
    sums[...] = jnp.zeros_like(sums)

    for place in (1, 2, 3):
        wait_bytes(images.at[pl.ds(0, 2 * HALF)], image_rs.at[place])
        pass_images(place)
    text_copies[2, 0].wait_recv()
    send_text(2, -1, 0, HALF, 6)
    send_text(2, -2, 0, HALF, 7)
    text_copies[6, HALF].wait_recv()
    send_text(6, 1, HALF, HALF, 8)
    send_text(6, 2, HALF, HALF, 9)
    text_copies[2, HALF].wait_recv()
    send_text(2, -1, HALF, HALF, 10)
    text_copies[6, 0].wait_recv()
    send_text(6, 1, 0, HALF, 11)
    hand_text(2)
    hand_text(6)

    def pairs(products, first, second):
        rows = slice(first * GROUP, first * GROUP + GROUP)
        cols = slice(second * GROUP, second * GROUP + GROUP)
        grown = jnp.exp2(products * temper2 + offset2)
        above = 1.0 + grown
        slope = grown / above
        packed = above[0:128] * above[128:256]
        packed = packed[0:64] * packed[64:128]
        packed = packed[0:32] * packed[32:64]
        loss = fold(jnp.log(packed))
        if first == 0 and second == 0:
            row = lax.broadcasted_iota(jnp.int32, (GROUP, GROUP), 0)
            col = lax.broadcasted_iota(jnp.int32, (GROUP, GROUP), 1)
            upper = (row == col) & (row < HALF)
            lower = (row - LINE + HALF == col) & (row >= LINE) & (row < LINE + HALF)
            matched = jnp.where(upper | lower, 1.0, 0.0)
            slope = slope - matched
            loss = loss - fold(matched * (products * temper + offset))
        slope_b = slope.astype(jnp.bfloat16)
        slopes[rows, cols] = slope_b
        slopes_t[cols, rows] = slope_b.T
        return loss, fold(slope), fold(slope * products)

    def tiles(*places):
        products = [
            jnp.dot(
                images[first * GROUP : first * GROUP + GROUP, :],
                texts_t[:, second * GROUP : second * GROUP + GROUP],
                preferred_element_type=jnp.float32,
            )
            for first, second in places
        ]
        shares = [pairs(product, *place) for product, place in zip(products, places)]
        for n in range(3):
            sums[n] += sum(share[n] for share in shares)

    def wait_lines(line):
        wait_bytes(images.at[pl.ds(line * GROUP, GROUP)], lines_rs.at[line])

    def turn_texts(group):
        wait_bytes(texts.at[pl.ds(group * GROUP + LINE, LINE)], pair_rs.at[group])
        rows = slice(group * GROUP, group * GROUP + GROUP)
        texts_t[:, rows] = texts[rows, :].T

    def spread(stage, values, peers):
        found_out[stage] = values
        first = FOUND[stage]
        for n, peer in enumerate(peers):
            send(found_out.at[stage], found_in.at[first + n], f_ss.at[0], f_rs.at[stage], peer)

    def collect(stage, values):
        first, end = FOUND[stage], FOUND[stage + 1]
        wait_bytes(found_in.at[pl.ds(first, end - first)], f_rs.at[stage])
        for n in range(first, end):
            values = values + found_in[n]
        return values

    row = lax.broadcasted_iota(jnp.int32, (8, 128), 0)
    mid_copies, gp_copies = {}, {}

    def image_grads(line):
        rows = slice(line * GROUP, line * GROUP + GROUP)
        part = temper3 * jnp.dot(slopes[rows, :], texts[...], preferred_element_type=jnp.float32)
        if line == 0:
            image_own[...] = part
        else:
            image_part[rows, :] = part.astype(jnp.bfloat16)

    def send_line(line, place):
        first, back = place * HALF, AROUND_BACK[line]
        for half in (0, 1):
            send(
                image_part.at[pl.ds(image_row(half, line, place), HALF)],
                image_in.at[half, back, pl.ds(first, HALF)],
                line_ss.at[0], line_rs.at[half, place], axes[1 - half][line],
            )

    def line_sum(half, place):
        first = place * HALF
        row = half * LINE + first
        part = image_own[row : row + HALF, :]
        wait_bytes(image_in.at[half, pl.ds(1, 3), pl.ds(first, HALF)], line_rs.at[half, place])
        for line in (3, 1, 2):
            part = part + wide(image_in[half, line, first : first + HALF, :])
        return part

    def text_grads(group):
        rows = slice(group * GROUP, group * GROUP + GROUP)
        part = temper3 * jnp.dot(slopes_t[rows, :], images[...], preferred_element_type=jnp.float32)
        own = slice(group * LINE, group * LINE + LINE)
        text_own[own, :] = part[0:LINE]
        pair_part[own, :] = part[LINE:GROUP].astype(jnp.bfloat16)
        gp_copies[group] = send(
            pair_part.at[own], pair_in.at[own], gp_ss.at[0], gp_rs.at[group], twin
        )

    def own_rows(block, first=0, count=ROWS):
        place = COLUMN.index(block)
        return slice(place * ROWS + first, place * ROWS + first + count)

    def text_sums(group):
        gp_copies[group].wait_recv()
        own = slice(group * LINE, group * LINE + LINE)
        part = text_own[own, :] + wide(pair_in[own, :])
        text_own[own, :] = part
        text_part[own, :] = part.astype(jnp.bfloat16)

    def send_mid(block, step, first, count, slot):
        mid_copies[slot] = send(
            text_part.at[own_rows(block, first, count)], text_mid.at[slot, pl.ds(first, count)],
            mid_ss.at[0], mid_rs.at[slot], column[step % 8],
        )

    def send_share(block, slot):
        send(
            text_part.at[own_rows(block)], text_in.at[slot], gt_ss.at[0], gt_rs.at[0], column[block]
        )

    def add_mid(block, near, far, first, slot):
        mid_copies[near].wait_recv()
        part = text_own[own_rows(block), :] + wide(text_mid[near])
        mid_copies[far].wait_recv()
        more = part[first : first + HALF] + wide(text_mid[far, first : first + HALF, :])
        part = jnp.concatenate([more, part[HALF:]] if first == 0 else [part[:HALF], more], axis=0)
        text_part[own_rows(block), :] = part.astype(jnp.bfloat16)
        send_share(block, slot)

    for block in (1, 7):
        text_copies[block, 0].wait_recv()
        hand_text(block)
    turn_texts(0)
    turn_texts(1)
    tiles((0, 0), (0, 1))
    wait_lines(1)
    wait_lines(2)
    tiles((1, 0), (1, 1), (2, 0), (2, 1))
    for block in (3, 5):
        for first in (0, HALF):
            text_copies[block, first].wait_recv()
        hand_text(block)
    wait_lines(3)
    tiles((3, 0), (3, 1))
    for first in (0, HALF):
        text_copies[4, first].wait_recv()
    hand_text(4)
    turn_texts(3)
    tiles((3, 3), (1, 3), (2, 3), (0, 3))
    turn_texts(2)
    tiles((3, 2), (1, 2), (2, 2), (0, 2))

    lane_sums = [jnp.sum(sums[n], keepdims=True) for n in range(3)]
    found = jnp.where(row == 0, lane_sums[0], jnp.where(row == 1, lane_sums[1], lane_sums[2]))
    spread(0, found, [twin])
    image_grads(3)
    for place in (3, 1, 2):
        send_line(3, place)
    text_grads(3)
    image_grads(1)
    for place in (3, 1, 2):
        send_line(1, place)
    found = collect(0, found)
    spread(1, found, list(column.values()))
    text_grads(2)
    text_sums(3)
    send_mid(3, 1, 0, ROWS, 0)
    send_mid(5, -1, 0, ROWS, 1)
    image_grads(2)
    for place in (3, 1, 2):
        send_line(2, place)
    for line in (3, 1, 2):
        send_line(line, 0)
    text_sums(2)
    send_mid(4, 2, 0, HALF, 2)
    send_mid(4, -2, HALF, HALF, 3)
    text_grads(1)
    text_grads(0)
    image_grads(0)
    text_sums(1)
    send_share(7, 0)
    text_sums(0)
    send_share(1, 1)
    found = collect(1, found)
    spread(2, found, axes[1][1:])
    add_mid(2, 0, 2, 0, 2)
    add_mid(6, 1, 3, HALF, 3)

    for place in (3, 1, 2):
        for half in (0, 1):
            first, back = place * HALF - HALF, AROUND_BACK[place]
            image_mid[half, first : first + HALF, :] = line_sum(half, place).astype(jnp.bfloat16)
            send(
                image_mid.at[half, pl.ds(first, HALF)], image_last.at[half, back],
                last_ss.at[0], last_rs.at[half], axes[half][place],
            )
    found = collect(2, found)
    spread(3, found, axes[0][1:])
    ends = [line_sum(half, 0) for half in (0, 1)]

    total = text_own[0:ROWS, :]
    wait_bytes(text_in, gt_rs.at[0])
    for slot in range(4):
        total = total + wide(text_in[slot])
    total_text_ref[...] = total

    for half in (0, 1):
        total = ends[half]
        wait_bytes(image_last.at[half, pl.ds(1, 3)], last_rs.at[half])
        for place in (1, 2, 3):
            total = total + wide(image_last[half, place])
        rows = slice(half * HALF, half * HALF + HALF)
        total_image_ref[rows, :] = total

    found = collect(3, found) * (1.0 / float(TOTAL) ** 2)
    lane = lax.broadcasted_iota(jnp.int32, (8, 128), 1)
    scale, slope = found[2:3] * temper[:, 0:128], found[1:2]
    scalars_ref[...] = jnp.where(row == 0, found, jnp.where(lane == 0, scale, slope))

    wait_bytes(images.at[0 : 30 * HALF], image_ss.at[0])
    wait_bytes(texts.at[0 : 7 * ROWS], text_ss.at[0])
    wait_bytes(texts.at[0 : 8 * ROWS], pair_ss.at[0])
    wait_bytes(image_part.at[0 : 6 * LINE], line_ss.at[0])
    wait_bytes(image_mid, last_ss.at[0])
    wait_bytes(text_part.at[0 : 4 * ROWS], gt_ss.at[0])
    wait_bytes(text_part.at[0 : 3 * ROWS], mid_ss.at[0])
    wait_bytes(pair_part, gp_ss.at[0])
    wait_bytes(found_in.at[0 : FOUND[4]], f_ss.at[0])


def finish(image_ref, text_ref, total_image_ref, total_text_ref, scalars_ref, mean_ref, grad_image_ref, grad_text_ref, pair_ref):
    grad_image_ref[...] = back_rows(wide(image_ref[...]), total_image_ref[...])
    grad_text_ref[...] = back_rows(wide(text_ref[...]), total_text_ref[...])
    mean_ref[...] = scalars_ref[0, 0:1]
    pair_ref[...] = scalars_ref[1, 0:2]


def local(image_emb, text_emb, log_temp, bias):
    bf16, f32 = jnp.bfloat16, jnp.float32
    vmem, hbm = pl.BlockSpec(memory_space=pltpu.VMEM), pl.BlockSpec(memory_space=pltpu.HBM)
    dma = pltpu.SemaphoreType.DMA
    total_image, total_text, scalars = pl.pallas_call(
        kernel,
        out_shape=(
            jax.ShapeDtypeStruct((ROWS, WIDTH), f32),
            jax.ShapeDtypeStruct((ROWS, WIDTH), f32),
            jax.ShapeDtypeStruct((8, 128), f32),
        ),
        in_specs=[hbm] * 4,
        out_specs=(vmem, vmem, vmem),
        scratch_shapes=[
            pltpu.SMEM((1,), f32),
            pltpu.SMEM((1,), f32),
            pltpu.VMEM((ROWS, WIDTH), bf16),
            pltpu.VMEM((ROWS, WIDTH), bf16),
            pltpu.VMEM((16 * ROWS, WIDTH), bf16),
            pltpu.VMEM((16 * ROWS, WIDTH), bf16),
            pltpu.VMEM((WIDTH, 16 * ROWS), bf16),
            pltpu.VMEM((16 * ROWS, 16 * ROWS), bf16),
            pltpu.VMEM((16 * ROWS, 16 * ROWS), bf16),
            pltpu.VMEM((3, 8, 256), f32),
            pltpu.VMEM((16 * ROWS, WIDTH), bf16),
            pltpu.VMEM((GROUP, WIDTH), f32),
            pltpu.VMEM((2, 4, LINE, WIDTH), bf16),
            pltpu.VMEM((2, LINE - HALF, WIDTH), bf16),
            pltpu.VMEM((2, 4, HALF, WIDTH), bf16),
            pltpu.VMEM((8 * ROWS, WIDTH), bf16),
            pltpu.VMEM((8 * ROWS, WIDTH), f32),
            pltpu.VMEM((4, ROWS, WIDTH), bf16),
            pltpu.VMEM((8 * ROWS, WIDTH), bf16),
            pltpu.VMEM((8 * ROWS, WIDTH), bf16),
            pltpu.VMEM((4, ROWS, WIDTH), bf16),
            pltpu.VMEM((14, 8, 128), f32),
            pltpu.VMEM((4, 8, 128), f32),
            dma((4,)),
            dma((1,)), dma((4,)), dma((4,)), dma((1,)), dma((12,)), dma((1,)), dma((4,)),
            dma((1,)), dma((2, 4)), dma((1,)), dma((2,)), dma((1,)), dma((1,)),
            dma((1,)), dma((4,)), dma((1,)), dma((4,)), dma((1,)), dma((4,)),
        ],
        compiler_params=pltpu.CompilerParams(
            collective_id=0, has_side_effects=True, vmem_limit_bytes=56 * 1024 * 1024
        ),
    )(image_emb, text_emb, log_temp, bias)
    mean_loss, grad_image, grad_text, scalar_grads = pl.pallas_call(
        finish,
        out_shape=(
            jax.ShapeDtypeStruct((1,), f32),
            jax.ShapeDtypeStruct((ROWS, WIDTH), f32),
            jax.ShapeDtypeStruct((ROWS, WIDTH), f32),
            jax.ShapeDtypeStruct((2,), f32),
        ),
        in_specs=[vmem] * 5,
        out_specs=(vmem,) * 4,
    )(image_emb, text_emb, total_image, total_text, scalars)
    return (mean_loss, grad_image, grad_text, scalar_grads)


def solution(mesh):
    placed = (P(("blk", "narrow"), None), P(("blk", "narrow"), None), P(), P())
    return jax.shard_map(
        local,
        mesh=mesh,
        in_specs=placed,
        out_specs=(P(), P(("blk", "narrow"), None), P(("blk", "narrow"), None), P()),
        check_vma=False,
    )
```

```python
import math

import jax
import jax.numpy as jnp
from jax import lax
from jax.experimental import pallas as pl
from jax.experimental.pallas import tpu as pltpu
from jax.sharding import PartitionSpec as P

MESH = pl.DeviceIdType.MESH
ROWS, WIDTH = 64, 768
HALF, LINE, GROUP = ROWS // 2, 2 * ROWS, 4 * ROWS
TOTAL = 16384
LOG2E = math.log2(math.e)

AROUND = (0, 1, 3, 2)
AROUND_BACK = tuple(AROUND.index(-d % 4) for d in AROUND)
COLUMN = (0, 1, 7, 6, 2, 4, 3, 5)
FOUND = (0, 1, 8, 11, 14)
COLUMN_BACK = tuple(COLUMN.index(-d % 8) for d in COLUMN)


def image_row(half, line, place):
    return line * GROUP + half * LINE + place * HALF


def text_row(other, place):
    return (place // 2 * 4 + other * 2 + place % 2) * ROWS


def row_scale(values):
    return lax.rsqrt(jnp.sum(values * values, axis=-1, keepdims=True) + 1e-06)


def back_rows(values, upstream):
    inverse = row_scale(values)
    unit = values * inverse
    return inverse * (upstream - unit * jnp.sum(unit * upstream, axis=-1, keepdims=True))


def fold(values):
    return jnp.sum(jnp.reshape(values, (values.shape[0] // 8, 8, values.shape[1])), axis=0)


def wide(ref):
    return ref.astype(jnp.float32)


def kernel(
    image_hbm, text_hbm, temp_hbm, bias_hbm,
    grad_image_out, grad_text_out, scalars_ref,
    temp_ref, bias_ref, image_ref, text_ref, images, texts, texts_t, slopes, slopes_t, sums,
    image_part, image_own, image_in, image_mid, image_last,
    text_part, text_own, text_in, pair_part, pair_in, text_mid, found_in, found_out,
    load, image_ss, image_rs, lines_rs, text_ss, text_rs, pair_ss, pair_rs,
    line_ss, line_rs, last_ss, last_rs, gt_ss, gt_rs, mid_ss, mid_rs, gp_ss, gp_rs, f_ss, f_rs,
):
    blk, narrow = lax.axis_index("blk"), lax.axis_index("narrow")
    x, core = lax.div(blk, 4), lax.rem(blk, 2)
    y = lax.rem(lax.div(blk, 2), 2) * 2 + lax.div(narrow, 8)
    z = lax.rem(narrow, 8)

    def device(dx, dy, dz, other):
        px, py, pz = lax.rem(x + dx, 4), lax.rem(y + dy, 4), lax.rem(z + dz, 8)
        pc = lax.rem(core + other, 2)
        return (px * 4 + lax.div(py, 2) * 2 + pc, lax.rem(py, 2) * 8 + pz)

    axes = ([device(d, 0, 0, 0) for d in AROUND], [device(0, d, 0, 0) for d in AROUND])
    column = {d: device(0, 0, d, 0) for d in range(1, 8)}
    twin = device(0, 0, 0, 1)

    loads = [
        pltpu.make_async_copy(image_hbm, image_ref, load.at[0]),
        pltpu.make_async_copy(text_hbm, text_ref, load.at[1]),
        pltpu.make_async_copy(temp_hbm, temp_ref, load.at[2]),
        pltpu.make_async_copy(bias_hbm, bias_ref, load.at[3]),
    ]
    for copy in loads:
        copy.start()
    barrier = pltpu.get_barrier_semaphore()
    peers = [axes[0][3], axes[1][3], *axes[0][1:3], *axes[1][1:3], *column.values(), twin]
    for peer in peers:
        pl.semaphore_signal(barrier, inc=1, device_id=peer, device_id_type=MESH)

    loads[0].wait()
    image = wide(image_ref[...])
    image = (image * row_scale(image)).astype(jnp.bfloat16)
    for half in (0, 1):
        row = image_row(half, 0, 0)
        images[row : row + HALF, :] = image[half * HALF : half * HALF + HALF]

    pl.semaphore_wait(barrier, len(peers))

    def send(src, dst, send_sem, recv_sem, peer):
        copy = pltpu.make_async_remote_copy(
            src_ref=src, dst_ref=dst, send_sem=send_sem, recv_sem=recv_sem,
            device_id=peer, device_id_type=MESH,
        )
        copy.start()
        return copy

    def wait_bytes(ref, sem):
        pltpu.make_async_copy(ref, ref, sem).wait()

    text_copies = {}

    def first_image(half, place):
        back = AROUND_BACK[place]
        send(
            images.at[pl.ds(image_row(half, 0, 0), HALF)],
            images.at[pl.ds(image_row(half, 0, back), HALF)],
            image_ss.at[0], image_rs.at[back], axes[half][place],
        )

    def pass_images(place):
        for line in (1, 2, 3):
            back = AROUND_BACK[line]
            for half in (0, 1):
                send(
                    images.at[pl.ds(image_row(half, 0, place), HALF)],
                    images.at[pl.ds(image_row(half, back, place), HALF)],
                    image_ss.at[0], lines_rs.at[back], axes[1 - half][line],
                )

    def send_text(block, step, first, count, slot):
        source, target = text_row(0, COLUMN.index(block)), text_row(0, COLUMN.index((block - step) % 8))
        text_copies[(block - step) % 8, first] = send(
            texts.at[pl.ds(source + first, count)], texts.at[pl.ds(target + first, count)],
            text_ss.at[0], text_rs.at[slot], column[step % 8],
        )

    def hand_text(block):
        place = COLUMN.index(block)
        send(
            texts.at[pl.ds(text_row(0, place), ROWS)], texts.at[pl.ds(text_row(1, place), ROWS)],
            pair_ss.at[0], pair_rs.at[place // 2], twin,
        )

    for place in (1, 2, 3):
        for half in (0, 1):
            first_image(half, place)
    loads[1].wait()
    text = wide(text_ref[...])
    texts[0:ROWS, :] = (text * row_scale(text)).astype(jnp.bfloat16)
    send_text(0, 2, HALF, HALF, 0)
    send_text(0, -2, 0, HALF, 1)
    send_text(0, 2, 0, HALF, 2)
    send_text(0, -2, HALF, HALF, 3)
    hand_text(0)
    pass_images(0)
    send_text(0, 1, 0, ROWS, 4)
    send_text(0, -1, 0, ROWS, 5)

    for copy in loads[2:]:
        copy.wait()
    temper = jnp.exp(jnp.full((1, 256), temp_ref[0], jnp.float32))
    offset = jnp.full((1, 256), bias_ref[0], jnp.float32)
    temper2, offset2 = temper * LOG2E, offset * LOG2E
    temper3 = jnp.concatenate([temper] * 3, axis=1)
    sums[...] = jnp.zeros_like(sums)

    for place in (1, 2, 3):
        wait_bytes(images.at[pl.ds(0, 2 * HALF)], image_rs.at[place])
        pass_images(place)
    text_copies[2, 0].wait_recv()
    send_text(2, -1, 0, HALF, 6)
    send_text(2, -2, 0, HALF, 7)
    text_copies[6, HALF].wait_recv()
    send_text(6, 1, HALF, HALF, 8)
    send_text(6, 2, HALF, HALF, 9)
    text_copies[2, HALF].wait_recv()
    send_text(2, -1, HALF, HALF, 10)
    text_copies[6, 0].wait_recv()
    send_text(6, 1, 0, HALF, 11)
    hand_text(2)
    hand_text(6)

    def pairs(products, first, second):
        rows = slice(first * GROUP, first * GROUP + GROUP)
        cols = slice(second * GROUP, second * GROUP + GROUP)
        grown = jnp.exp2(products * temper2 + offset2)
        above = 1.0 + grown
        slope = grown / above
        packed = above[0:128] * above[128:256]
        packed = packed[0:64] * packed[64:128]
        packed = packed[0:32] * packed[32:64]
        loss = fold(jnp.log(packed))
        if first == 0 and second == 0:
            row = lax.broadcasted_iota(jnp.int32, (GROUP, GROUP), 0)
            col = lax.broadcasted_iota(jnp.int32, (GROUP, GROUP), 1)
            upper = (row == col) & (row < HALF)
            lower = (row - LINE + HALF == col) & (row >= LINE) & (row < LINE + HALF)
            matched = jnp.where(upper | lower, 1.0, 0.0)
            slope = slope - matched
            loss = loss - fold(matched * (products * temper + offset))
        slope_b = slope.astype(jnp.bfloat16)
        slopes[rows, cols] = slope_b
        slopes_t[cols, rows] = slope_b.T
        return loss, fold(slope), fold(slope * products)

    def tiles(*places):
        products = [
            jnp.dot(
                images[first * GROUP : first * GROUP + GROUP, :],
                texts_t[:, second * GROUP : second * GROUP + GROUP],
                preferred_element_type=jnp.float32,
            )
            for first, second in places
        ]
        shares = [pairs(product, *place) for product, place in zip(products, places)]
        for n in range(3):
            sums[n] += sum(share[n] for share in shares)

    def wait_lines(line):
        wait_bytes(images.at[pl.ds(line * GROUP, GROUP)], lines_rs.at[line])

    def turn_texts(group):
        wait_bytes(texts.at[pl.ds(group * GROUP + LINE, LINE)], pair_rs.at[group])
        rows = slice(group * GROUP, group * GROUP + GROUP)
        texts_t[:, rows] = texts[rows, :].T

    def spread(stage, values, peers):
        found_out[stage] = values
        first = FOUND[stage]
        for n, peer in enumerate(peers):
            send(found_out.at[stage], found_in.at[first + n], f_ss.at[0], f_rs.at[stage], peer)

    def collect(stage, values):
        first, end = FOUND[stage], FOUND[stage + 1]
        wait_bytes(found_in.at[pl.ds(first, end - first)], f_rs.at[stage])
        for n in range(first, end):
            values = values + found_in[n]
        return values

    row = lax.broadcasted_iota(jnp.int32, (8, 128), 0)
    mid_copies, gp_copies = {}, {}

    def image_grads(line):
        rows = slice(line * GROUP, line * GROUP + GROUP)
        part = temper3 * jnp.dot(slopes[rows, :], texts[...], preferred_element_type=jnp.float32)
        if line == 0:
            image_own[...] = part
        else:
            image_part[rows, :] = part.astype(jnp.bfloat16)

    def send_line(line, place):
        first, back = place * HALF, AROUND_BACK[line]
        for half in (0, 1):
            send(
                image_part.at[pl.ds(image_row(half, line, place), HALF)],
                image_in.at[half, back, pl.ds(first, HALF)],
                line_ss.at[0], line_rs.at[half, place], axes[1 - half][line],
            )

    def line_sum(half, place):
        first = place * HALF
        row = half * LINE + first
        part = image_own[row : row + HALF, :]
        wait_bytes(image_in.at[half, pl.ds(1, 3), pl.ds(first, HALF)], line_rs.at[half, place])
        for line in (3, 1, 2):
            part = part + wide(image_in[half, line, first : first + HALF, :])
        return part

    def text_grads(group):
        rows = slice(group * GROUP, group * GROUP + GROUP)
        part = temper3 * jnp.dot(slopes_t[rows, :], images[...], preferred_element_type=jnp.float32)
        own = slice(group * LINE, group * LINE + LINE)
        text_own[own, :] = part[0:LINE]
        pair_part[own, :] = part[LINE:GROUP].astype(jnp.bfloat16)
        gp_copies[group] = send(
            pair_part.at[own], pair_in.at[own], gp_ss.at[0], gp_rs.at[group], twin
        )

    def own_rows(block, first=0, count=ROWS):
        place = COLUMN.index(block)
        return slice(place * ROWS + first, place * ROWS + first + count)

    def text_sums(group):
        gp_copies[group].wait_recv()
        own = slice(group * LINE, group * LINE + LINE)
        part = text_own[own, :] + wide(pair_in[own, :])
        text_own[own, :] = part
        text_part[own, :] = part.astype(jnp.bfloat16)

    def send_mid(block, step, first, count, slot):
        mid_copies[slot] = send(
            text_part.at[own_rows(block, first, count)], text_mid.at[slot, pl.ds(first, count)],
            mid_ss.at[0], mid_rs.at[slot], column[step % 8],
        )

    def send_share(block, slot):
        send(
            text_part.at[own_rows(block)], text_in.at[slot], gt_ss.at[0], gt_rs.at[0], column[block]
        )

    def add_mid(block, near, far, first, slot):
        mid_copies[near].wait_recv()
        part = text_own[own_rows(block), :] + wide(text_mid[near])
        mid_copies[far].wait_recv()
        more = part[first : first + HALF] + wide(text_mid[far, first : first + HALF, :])
        part = jnp.concatenate([more, part[HALF:]] if first == 0 else [part[:HALF], more], axis=0)
        text_part[own_rows(block), :] = part.astype(jnp.bfloat16)
        send_share(block, slot)

    for block in (1, 7):
        text_copies[block, 0].wait_recv()
        hand_text(block)
    turn_texts(0)
    turn_texts(1)
    tiles((0, 0), (0, 1))
    wait_lines(1)
    wait_lines(2)
    tiles((1, 0), (1, 1), (2, 0), (2, 1))
    for block in (3, 5):
        for first in (0, HALF):
            text_copies[block, first].wait_recv()
        hand_text(block)
    wait_lines(3)
    tiles((3, 0), (3, 1))
    for first in (0, HALF):
        text_copies[4, first].wait_recv()
    hand_text(4)
    turn_texts(3)
    tiles((3, 3), (1, 3), (2, 3), (0, 3))
    turn_texts(2)
    tiles((3, 2), (1, 2), (2, 2), (0, 2))

    lane_sums = [jnp.sum(sums[n], keepdims=True) for n in range(3)]
    found = jnp.where(row == 0, lane_sums[0], jnp.where(row == 1, lane_sums[1], lane_sums[2]))
    spread(0, found, [twin])
    image_grads(3)
    for place in (3, 1, 2):
        send_line(3, place)
    text_grads(3)
    image_grads(1)
    for place in (3, 1, 2):
        send_line(1, place)
    found = collect(0, found)
    spread(1, found, list(column.values()))
    text_grads(2)
    text_sums(3)
    send_mid(3, 1, 0, ROWS, 0)
    send_mid(5, -1, 0, ROWS, 1)
    image_grads(2)
    for place in (3, 1, 2):
        send_line(2, place)
    for line in (3, 1, 2):
        send_line(line, 0)
    text_sums(2)
    send_mid(4, 2, 0, HALF, 2)
    send_mid(4, -2, HALF, HALF, 3)
    text_grads(1)
    text_grads(0)
    image_grads(0)
    text_sums(1)
    send_share(7, 0)
    text_sums(0)
    send_share(1, 1)
    found = collect(1, found)
    spread(2, found, axes[1][1:])
    add_mid(2, 0, 2, 0, 2)
    add_mid(6, 1, 3, HALF, 3)

    for place in (3, 1, 2):
        for half in (0, 1):
            first, back = place * HALF - HALF, AROUND_BACK[place]
            image_mid[half, first : first + HALF, :] = line_sum(half, place).astype(jnp.bfloat16)
            send(
                image_mid.at[half, pl.ds(first, HALF)], image_last.at[half, back],
                last_ss.at[0], last_rs.at[half], axes[half][place],
            )
    found = collect(2, found)
    spread(3, found, axes[0][1:])
    ends = [line_sum(half, 0) for half in (0, 1)]

    total = text_own[0:ROWS, :]
    wait_bytes(text_in, gt_rs.at[0])
    for slot in range(4):
        total = total + wide(text_in[slot])
    grad_text_out[...] = back_rows(wide(text_ref[...]), total)

    for half in (0, 1):
        total = ends[half]
        wait_bytes(image_last.at[half, pl.ds(1, 3)], last_rs.at[half])
        for place in (1, 2, 3):
            total = total + wide(image_last[half, place])
        rows = slice(half * HALF, half * HALF + HALF)
        grad_image_out[rows, :] = back_rows(wide(image_ref[rows, :]), total)

    found = collect(3, found) * (1.0 / float(TOTAL) ** 2)
    lane = lax.broadcasted_iota(jnp.int32, (8, 128), 1)
    scale, slope = found[2:3] * temper[:, 0:128], found[1:2]
    scalars_ref[...] = jnp.where(row == 0, found, jnp.where(lane == 0, scale, slope))

    wait_bytes(images.at[0 : 30 * HALF], image_ss.at[0])
    wait_bytes(texts.at[0 : 7 * ROWS], text_ss.at[0])
    wait_bytes(texts.at[0 : 8 * ROWS], pair_ss.at[0])
    wait_bytes(image_part.at[0 : 6 * LINE], line_ss.at[0])
    wait_bytes(image_mid, last_ss.at[0])
    wait_bytes(text_part.at[0 : 4 * ROWS], gt_ss.at[0])
    wait_bytes(text_part.at[0 : 3 * ROWS], mid_ss.at[0])
    wait_bytes(pair_part, gp_ss.at[0])
    wait_bytes(found_in.at[0 : FOUND[4]], f_ss.at[0])


def finish(image_in, text_in, scalars_ref, mean_ref, image_out, text_out, pair_ref):
    image_out[...] = image_in[...]
    text_out[...] = text_in[...]
    mean_ref[...] = scalars_ref[0, 0:1]
    pair_ref[...] = scalars_ref[1, 0:2]


def local(image_emb, text_emb, log_temp, bias):
    bf16, f32 = jnp.bfloat16, jnp.float32
    vmem, hbm = pl.BlockSpec(memory_space=pltpu.VMEM), pl.BlockSpec(memory_space=pltpu.HBM)
    dma = pltpu.SemaphoreType.DMA
    grad_image, grad_text, scalars = pl.pallas_call(
        kernel,
        out_shape=(
            jax.ShapeDtypeStruct((ROWS, WIDTH), f32),
            jax.ShapeDtypeStruct((ROWS, WIDTH), f32),
            jax.ShapeDtypeStruct((8, 128), f32),
        ),
        in_specs=[hbm] * 4,
        out_specs=(vmem, vmem, vmem),
        scratch_shapes=[
            pltpu.SMEM((1,), f32),
            pltpu.SMEM((1,), f32),
            pltpu.VMEM((ROWS, WIDTH), bf16),
            pltpu.VMEM((ROWS, WIDTH), bf16),
            pltpu.VMEM((16 * ROWS, WIDTH), bf16),
            pltpu.VMEM((16 * ROWS, WIDTH), bf16),
            pltpu.VMEM((WIDTH, 16 * ROWS), bf16),
            pltpu.VMEM((16 * ROWS, 16 * ROWS), bf16),
            pltpu.VMEM((16 * ROWS, 16 * ROWS), bf16),
            pltpu.VMEM((3, 8, 256), f32),
            pltpu.VMEM((16 * ROWS, WIDTH), bf16),
            pltpu.VMEM((GROUP, WIDTH), f32),
            pltpu.VMEM((2, 4, LINE, WIDTH), bf16),
            pltpu.VMEM((2, LINE - HALF, WIDTH), bf16),
            pltpu.VMEM((2, 4, HALF, WIDTH), bf16),
            pltpu.VMEM((8 * ROWS, WIDTH), bf16),
            pltpu.VMEM((8 * ROWS, WIDTH), f32),
            pltpu.VMEM((4, ROWS, WIDTH), bf16),
            pltpu.VMEM((8 * ROWS, WIDTH), bf16),
            pltpu.VMEM((8 * ROWS, WIDTH), bf16),
            pltpu.VMEM((4, ROWS, WIDTH), bf16),
            pltpu.VMEM((14, 8, 128), f32),
            pltpu.VMEM((4, 8, 128), f32),
            dma((4,)),
            dma((1,)), dma((4,)), dma((4,)), dma((1,)), dma((12,)), dma((1,)), dma((4,)),
            dma((1,)), dma((2, 4)), dma((1,)), dma((2,)), dma((1,)), dma((1,)),
            dma((1,)), dma((4,)), dma((1,)), dma((4,)), dma((1,)), dma((4,)),
        ],
        compiler_params=pltpu.CompilerParams(
            collective_id=0, has_side_effects=True, vmem_limit_bytes=56 * 1024 * 1024
        ),
    )(image_emb, text_emb, log_temp, bias)
    mean_loss, grad_image, grad_text, scalar_grads = pl.pallas_call(
        finish,
        out_shape=(
            jax.ShapeDtypeStruct((1,), f32),
            jax.ShapeDtypeStruct((ROWS, WIDTH), f32),
            jax.ShapeDtypeStruct((ROWS, WIDTH), f32),
            jax.ShapeDtypeStruct((2,), f32),
        ),
        in_specs=[vmem] * 3,
        out_specs=(vmem,) * 4,
    )(grad_image, grad_text, scalars)
    return (mean_loss, grad_image, grad_text, scalar_grads)


def solution(mesh):
    placed = (P(("blk", "narrow"), None), P(("blk", "narrow"), None), P(), P())
    return jax.shard_map(
        local,
        mesh=mesh,
        in_specs=placed,
        out_specs=(P(), P(("blk", "narrow"), None), P(("blk", "narrow"), None), P()),
        check_vma=False,
    )
```
